256 devices in a mesh: dp: 4 (over x), ctx: 16 (over z, core), tp: 4 (over y).
Axes of the slice: x: 4, y: 4, z: 8, core: 2. Of those that a mesh axis runs over, the one named last changes fastest.
Arguments:
- queries: bfloat16 [16384, 8192], P(('dp', 'ctx'), 'tp'), parts along dimension 0, may hold values from -50 to 50
- key_value_vectors: bfloat16 [16384, 2048], P(('dp', 'ctx'), 'tp'), parts along dimension 0, may hold values from -12 to 12
- out_weight: bfloat16 [8192, 4096], P('tp', 'ctx'), may hold values from -0.5 to 0.5
- doc_lengths: int32 [32], P('dp'), parts along dimension 0, may hold values from 1 to 1024, 4096 in all
- shard_of: int32 [16384], P(('dp', 'ctx')), parts along dimension 0, may hold values from 0 to 15, as said below
Outputs:
- output: bfloat16 [16384, 4096], P(('dp', 'ctx'), 'tp'), parts along dimension 0
The draws below stay inside these ranges and needn't reach their ends.
There are 4 independent parts, one for each index of `dp`. The reference program is written for one: setup_inputs(seed, part) draws one part's arguments, and reference() takes and returns one part's arrays. A program takes and returns all parts, laid end to end along the dimension named above; an argument that names none is the same for every part. Nothing has to cross between parts.
Inputs may be any that keep to these rules, and one draw needn't show every extreme that they name: `shard_of`: every aligned block of 16 positions has one shard; each shard holds exactly 256 tokens; the tokens of one context shard's input rows go to 8 shards, exactly 32 tokens to each.
All inputs are finite; a program needn't handle non-finite values.
Results may differ from the reference program's by a relative error of at most 0.0053.
Values may be sent and summed in bfloat16 or wider, within the bound.
A program may use at most 128 MiB of HBM per device.

```python
import math
import jax
import jax.numpy as jnp
import numpy as np
from jax import lax

QUERY_HEADS = 64
KEY_VALUE_HEADS = 8
HEAD_SIZE = 128
D_OUT = 4096
TOK_DEV = 256
DOCS = 8
WINDOW_TOKENS = 4096
BLK = 16


def draw_queries(key, part):
    key = jax.random.fold_in(key, 1)
    value_entries = jnp.clip(jax.random.normal(key, (WINDOW_TOKENS, QUERY_HEADS, HEAD_SIZE), jnp.float32), -6.0, 6.0)
    return value_entries.reshape(WINDOW_TOKENS, QUERY_HEADS * HEAD_SIZE).astype(jnp.bfloat16)


def draw_key_value_vectors(key, part):
    key = jax.random.fold_in(key, 2)
    value_entries = jnp.clip(jax.random.normal(key, (WINDOW_TOKENS, KEY_VALUE_HEADS, 2 * HEAD_SIZE), jnp.float32), -6.0, 6.0)
    return value_entries.reshape(WINDOW_TOKENS, KEY_VALUE_HEADS * 2 * HEAD_SIZE).astype(jnp.bfloat16)


def draw_shard_of(key, part):
    key = jax.random.fold_in(key, 5)
    order_key, turn_key, slot_key = jax.random.split(key, 3)
    shard_total = WINDOW_TOKENS // TOK_DEV
    targets = jax.random.permutation(order_key, shard_total)
    turns = jax.random.permutation(turn_key, shard_total)
    pair_steps = jnp.arange(shard_total // 2, dtype=jnp.int32)
    pair_dest = targets[(turns[:, None] + pair_steps[None, :]) % shard_total]
    slot_keys = jax.random.split(slot_key, shard_total)

    def one_source(one_key):
        return jax.random.permutation(one_key, shard_total)
    slot_perm = jax.vmap(one_source)(slot_keys)
    block_dest = jnp.take_along_axis(pair_dest, slot_perm // 2, axis=1)
    return jnp.repeat(block_dest.reshape(-1), BLK).astype(jnp.int32)


def level_of(stream_key, extent, cuts, low, largest):
    gain, own = 1.0, jax.random.fold_in(stream_key, 6)
    for axis_at, shards_of in cuts:
        heights = jnp.exp(jax.random.uniform(jax.random.fold_in(own, axis_at), (shards_of,), jnp.float32, low / len(cuts), largest / len(cuts)))
        gain = gain * jnp.repeat(heights, extent[axis_at] // shards_of).reshape([-1 if axis == axis_at else 1 for axis in range(len(extent))])
    return gain


def profile(count, total, bound, skew):
    portions = [(1 << 20) // math.isqrt(grade ** skew) + 1 for grade in range(2, count + 1)]
    spare, given = total - bound - (count - 1), [1] * (count - 1)
    while spare > 0:
        free = [i for i in range(count - 1) if given[i] < bound]
        mass, remaining = sum([portions[i] for i in free]), spare
        for i in free:
            extra = min(bound - given[i], max(1, remaining * portions[i] // mass), spare)
            given[i] = given[i] + extra
            spare = spare - extra
    return np.array([bound] + given)


def uneven(key, number_of, total, limit, lean):
    if number_of == 2:
        one = jax.random.randint(key, (), max(1, total - limit), min(limit, total - 1) + 1)
        return jnp.stack([one, total - one])
    sizes = jnp.asarray(profile(number_of, total, limit, lean), jnp.int32)
    couples = (number_of - 1) // 2
    giver, receiver = sizes[1:1 + 2 * couples:2], sizes[2:2 + 2 * couples:2]
    room = jnp.minimum(giver - 1, limit - receiver)
    moved = jax.random.randint(jax.random.fold_in(key, 1), (couples,), 0, 1 << 20) % (room + 1)
    sizes = sizes.at[1:1 + 2 * couples:2].set(giver - moved).at[2:2 + 2 * couples:2].set(receiver + moved)
    return sizes[jax.random.permutation(jax.random.fold_in(key, 2), number_of)]


def normal_values(key, shape, width, bound, shards=(), kind=jnp.bfloat16):
    values = jax.random.normal(key, shape, jnp.float32) * width
    if len(shards) > 0:
        values = level_of(key, shape, shards, -0.22, 0.18) * values
    return jnp.clip(values, min=-bound, max=bound).astype(kind)


def setup_inputs(seed: int = 0, part: int = 0) -> dict:
    key_list = jax.random.split(jax.random.key(seed), 6)
    own_keys = jax.random.split(jax.random.fold_in(key_list[5], part), 6)
    queries = draw_queries(jax.random.fold_in(jax.random.fold_in(key_list[5], part), 71), part)
    key_value_vectors = draw_key_value_vectors(jax.random.fold_in(jax.random.fold_in(key_list[5], part), 71), part)
    out_weight = normal_values(key_list[2], (QUERY_HEADS * HEAD_SIZE, D_OUT), HEAD_SIZE ** -0.5, 0.5, ((0, 4), (1, 16)))
    doc_lengths = uneven(own_keys[3], DOCS, WINDOW_TOKENS, WINDOW_TOKENS // 4, 2).astype(jnp.int32)
    shard_of = draw_shard_of(jax.random.fold_in(jax.random.fold_in(key_list[5], part), 71), part)
    return {"queries": queries, "key_value_vectors": key_value_vectors, "out_weight": out_weight, "doc_lengths": doc_lengths, "shard_of": shard_of}


def reference(queries, key_value_vectors, out_weight, doc_lengths, shard_of):
    positions = jnp.arange(WINDOW_TOKENS, dtype=jnp.int32)
    doc_ends = jnp.cumsum(doc_lengths)
    doc_of = lax.optimization_barrier(jnp.sum((positions[:, None] >= doc_ends[None, :]).astype(jnp.int32), axis=1))
    allowed = (doc_of[None, :] == doc_of[:, None]) & (positions[None, :] <= positions[:, None])
    query_heads = queries.reshape(WINDOW_TOKENS, QUERY_HEADS, HEAD_SIZE)
    paired_head_rows = key_value_vectors.reshape(WINDOW_TOKENS, KEY_VALUE_HEADS, 2 * HEAD_SIZE)
    score_scale = 1.0 / math.sqrt(HEAD_SIZE)

    def one_head(head_position_index):
        group_number_index = head_position_index // (QUERY_HEADS // KEY_VALUE_HEADS)
        query_rows = lax.dynamic_index_in_dim(query_heads, head_position_index, 1, False).astype(jnp.float32)
        pair_rows = lax.dynamic_index_in_dim(paired_head_rows, group_number_index, 1, False)
        key_rows = pair_rows[:, :HEAD_SIZE].astype(jnp.float32)
        value_rows = pair_rows[:, HEAD_SIZE:].astype(jnp.float32)
        scores = jnp.dot(query_rows, key_rows.T, precision=lax.Precision.HIGHEST) * score_scale
        scores = jnp.where(allowed, scores, -1e+30)
        row_peak = lax.optimization_barrier(jnp.max(scores, axis=1, keepdims=True))
        weights = jnp.exp(scores - row_peak)
        totals = lax.optimization_barrier(jnp.sum(weights, axis=1))
        rounded = lax.optimization_barrier(weights.astype(jnp.bfloat16)).astype(jnp.float32)
        mixed_out = jnp.dot(rounded, value_rows, precision=lax.Precision.HIGHEST) / totals[:, None]
        return mixed_out.astype(jnp.bfloat16)
    attended = lax.map(one_head, jnp.arange(QUERY_HEADS, dtype=jnp.int32))
    hidden = jnp.transpose(attended, (1, 0, 2)).reshape(WINDOW_TOKENS, QUERY_HEADS * HEAD_SIZE)
    packed_order = jnp.argsort(shard_of * WINDOW_TOKENS + positions)
    hidden_packed = hidden[packed_order]
    return jnp.dot(hidden_packed, out_weight, preferred_element_type=jnp.float32).astype(jnp.bfloat16)
```

```python
import math

import jax
import jax.numpy as jnp
from jax import lax
from jax.experimental import pallas as pl
from jax.experimental.pallas import tpu as pltpu
from jax.sharding import PartitionSpec as P

MESH = pl.DeviceIdType.MESH
BF = jnp.bfloat16
F32 = jnp.float32
HS = 128
TOK = 256
GH = 8
GW = GH * HS
NK = 5 * TOK
SCALE = math.log2(math.e) / math.sqrt(HS)
NZ = 8
NC = 16
NT = 4


def mult(value, of):
    return pl.multiple_of(value, of)


def kernel(
    q_ref, kv_ref, w_ref, meta_ref, len_ref, out_ref,
    qbuf, kvb, vo, bias, hbuf, wbuf, pbuf, rbuf, red, sbuf, gbuf, sel, take, mbuf, msm,
    loc, m_s, m_r, q_s, q_r, kv_s, kv_r, w_s, w_r, h_s, h_r, y_s, y_r, g_s, g_r,
):
    x = lax.axis_index("dp")
    c = lax.axis_index("ctx")
    t = lax.axis_index("tp")
    z = c // 2
    k = lax.rem(c, 2)
    xp = lax.rem(x, 2)
    xq = x + 1 - 2 * xp
    sib = c + 1 - 2 * k

    def remote(src, dst, send, recv, where):
        return pltpu.make_async_remote_copy(
            src_ref=src, dst_ref=dst, send_sem=send, recv_sem=recv, device_id=where, device_id_type=MESH
        )

    barrier = pltpu.get_barrier_semaphore()

    def greet_ctx(i, _):
        pl.semaphore_signal(barrier, inc=1, device_id={"ctx": lax.rem(c + i, NC)}, device_id_type=MESH)
        return 0

    lax.fori_loop(1, NC, greet_ctx, 0)
    for i in range(1, NT):
        pl.semaphore_signal(barrier, inc=1, device_id={"tp": lax.rem(t + i, NT)}, device_id_type=MESH)
    for i in range(NT):
        pl.semaphore_signal(barrier, inc=1, device_id={"dp": xq, "tp": lax.rem(t + i, NT)}, device_id_type=MESH)
    pl.semaphore_wait(barrier, NC - 1 + NT - 1 + NT)

    def kv_copy(i):
        if i == 0:
            g, slot, to = 1 - k, 4 + k, sib
        else:
            hop, g = (i + 1) // 2, (i + 1) % 2
            slot, to = 4 - 2 * hop + k, 2 * lax.rem(z + hop, NZ) + g
        return remote(
            kv_ref.at[:, pl.ds(mult(g * 256, 256), 256)], kvb.at[slot], kv_s.at[i], kv_r.at[slot], {"ctx": to}
        )

    def kv_arrival(slot):
        return remote(kvb.at[slot], kvb.at[slot], kv_s.at[0], kv_r.at[slot], {"ctx": sib})

    q_copy = remote(
        q_ref.at[:, pl.ds(mult((1 - k) * GW, GW), GW)], qbuf.at[k], q_s.at[0], q_r.at[0], {"ctx": sib}
    )
    q_arrival = remote(qbuf.at[1 - k], qbuf.at[1 - k], q_s.at[0], q_r.at[0], {"ctx": sib})

    def w_place(zz, j):
        return wbuf.at[zz // 2, pl.ds(j * 1024, 1024), pl.ds(mult(lax.rem(zz, 2) * 128, 128), 128)]

    def w_index(up, s, j):
        return ((0 if up else 3) + s - 1) * 2 + j

    def w_copy(up, s, j):
        zz = lax.rem(z + (NZ - s + 1 if up else s - 1), NZ)
        to = 2 * lax.rem(z + (1 if up else NZ - 1), NZ) + k
        n = w_index(up, s, j)
        src = w_ref.at[pl.ds(j * 1024, 1024), pl.ds(mult(xp * 128, 128), 128)] if s == 1 else w_place(zz, j)
        return remote(src, w_place(zz, j), w_s.at[n], w_r.at[n], {"ctx": to})

    def w_arrived(up, s, j):
        zz = lax.rem(z + (NZ - s if up else s), NZ)
        n = w_index(up, s, j)
        remote(w_place(zz, j), w_place(zz, j), w_s.at[n], w_r.at[n], {"ctx": sib}).wait_recv()
        if s < (3 if up else 4):
            w_copy(up, s + 1, j).start()

    local_copies = [
        pltpu.make_async_copy(q_ref.at[:, pl.ds(mult(k * GW, GW), GW)], qbuf.at[k], loc.at[0]),
        pltpu.make_async_copy(kv_ref.at[:, pl.ds(mult(k * 256, 256), 256)], kvb.at[4 + k], loc.at[1]),
        pltpu.make_async_copy(w_ref.at[:, pl.ds(mult(xp * 128, 128), 128)],
                              wbuf.at[z // 2, :, pl.ds(mult(lax.rem(z, 2) * 128, 128), 128)], loc.at[2]),
        pltpu.make_async_copy(meta_ref, mbuf.at[c], loc.at[3]),
    ]

    def m_copy(i):
        return remote(meta_ref, mbuf.at[c], m_s.at[i], m_r.at[i], {"ctx": lax.rem(c + i, NC)})

    for i in (1, 2, 3, 4, 0):
        kv_copy(i).start()
    q_copy.start()
    for copy in local_copies:
        copy.start()
    w_copy(False, 1, 0).start()
    w_copy(False, 1, 1).start()

    def m_send(i, _):
        m_copy(i).start()
        return 0

    lax.fori_loop(1, NC, m_send, 0)

    ends = []
    total = jnp.int32(0)
    for d in range(8):
        total = total + len_ref[d]
        ends.append(total)
    for s in range(2):
        base = z * 512 + s * 256
        rows = lax.broadcasted_iota(jnp.int32, (TOK, 1), 0)
        start = jnp.zeros((TOK, 1), jnp.int32)
        for e in ends:
            start = jnp.where(rows + base >= e, e, start)
        keys = lax.broadcasted_iota(jnp.int32, (TOK, NK), 1)
        seen = (keys <= rows + 1024) & (keys >= start - (base - 1024))
        bias[s] = jnp.where(seen, 0.0, -1e30).astype(F32)

    w_arrived(False, 1, 0)
    w_arrived(False, 1, 1)
    for i in (1, 2, 3, 4):
        kv_copy(i).wait_send()
    w_copy(True, 1, 0).start()
    w_copy(True, 1, 1).start()
    for copy in local_copies:
        copy.wait()
    q_arrival.wait_recv()
    kv_arrival(5 - k).wait_recv()
    for slot in range(4):
        kv_arrival(slot).wait_recv()
    vo[:, :, 0:HS] = kvb[:, :, HS:]
    vo[:, :, HS:] = jnp.ones((6, TOK, HS), BF)

    def h_lanes(j, kk):
        return pl.ds(mult(kk * GW + j * 256, 256), 256)

    def h_to_partner(j):
        return remote(hbuf.at[:, 0, :, h_lanes(j, k)], hbuf.at[:, 1, :, h_lanes(j, k)],
                      h_s.at[0, j], h_r.at[0, j], {"dp": xq})

    def h_to_sibling(j):
        return remote(hbuf.at[:, 0, :, h_lanes(j, k)], hbuf.at[:, 0, :, h_lanes(j, k)],
                      h_s.at[1, j], h_r.at[1, j], {"ctx": sib})

    def h_forward(j):
        return remote(hbuf.at[:, 1, :, h_lanes(j, k)], hbuf.at[:, 1, :, h_lanes(j, k)],
                      h_s.at[2, j], h_r.at[2, j], {"ctx": sib})

    def h_arrival(j, way):
        if way == 0:
            place = hbuf.at[:, 1, :, h_lanes(j, k)]
        else:
            place = hbuf.at[:, way - 1, :, h_lanes(j, 1 - k)]
        return remote(place, place, h_s.at[way, j], h_r.at[way, j], {"ctx": sib})

    def attend(j):
        def unit(i, _):
            s = i // 2
            h = 2 * j + lax.rem(i, 2)
            q = qbuf[s, :, pl.ds(mult(h * HS, HS), HS)]
            keys = kvb[pl.ds(s, 5), :, 0:HS].reshape(NK, HS)
            scores = lax.dot_general(q, keys, (((1,), (1,)), ((), ())), preferred_element_type=F32)
            scores = scores * SCALE + bias[s]
            peak = jnp.max(scores, axis=1, keepdims=True)
            weights = jnp.exp2(scores - peak).astype(BF)
            mixed = jnp.dot(weights, vo[pl.ds(s, 5)].reshape(NK, 2 * HS), preferred_element_type=F32)
            hbuf[s, 0, :, pl.ds(mult(k * GW + h * HS, HS), HS)] = (mixed[:, :HS] / mixed[:, HS:]).astype(BF)
            return 0

        lax.fori_loop(0, 4, unit, 0)
        h_to_partner(j).start()
        h_to_sibling(j).start()

    def h_pass_on(j):
        h_arrival(j, 0).wait_recv()
        h_forward(j).start()

    attend(0)
    w_arrived(False, 2, 0)
    attend(1)
    w_arrived(False, 2, 1)
    w_arrived(True, 1, 0)
    attend(2)
    attend(3)
    w_arrived(True, 1, 1)
    w_arrived(False, 3, 0)
    h_pass_on(0)
    h_pass_on(1)
    w_arrived(False, 3, 1)
    w_arrived(True, 2, 0)

    def m_wait(i, _):
        src = lax.rem(c + NC - i, NC)
        remote(mbuf.at[src], mbuf.at[src], m_s.at[i], m_r.at[i], {"ctx": sib}).wait_recv()
        return 0

    lax.fori_loop(1, NC, m_wait, 0)
    table = pltpu.make_async_copy(mbuf, msm, loc.at[4])
    table.start()
    table.wait()

    def choose(i, _):
        cc = lax.rem(c + i, NC)
        row = lax.broadcasted_iota(jnp.int32, (32, TOK), 0)
        column = lax.broadcasted_iota(jnp.int32, (32, TOK), 1)
        for s in range(2):
            one = msm[2 * z + s, 0, cc] * 16
            two = msm[2 * z + s, 0, NC + cc] * 16 - 16
            wanted = row + jnp.where(row < 16, one, two)
            sel[s, pl.ds(mult(i * 32, 32), 32), :] = jnp.where(column == wanted, 1.0, 0.0).astype(BF)
        return 0

    lax.fori_loop(0, NC, choose, 0)
    counts = []
    count = jnp.int32(0)
    for n in range(NC):
        count = count + msm[n, 0, 2 * NC + c]
        counts.append(count)

    def place(r, _):
        src = jnp.int32(0)
        for n in range(NC - 1):
            src = src + jnp.where(counts[n] <= r, 1, 0)
        row = lax.broadcasted_iota(jnp.int32, (32, 512), 0)
        column = lax.broadcasted_iota(jnp.int32, (32, 512), 1)
        take[pl.ds(mult(r * 32, 32), 32), :] = jnp.where(column == row + src * 32, 1.0, 0.0).astype(BF)
        return 0

    lax.fori_loop(0, 8, place, 0)

    w_arrived(True, 2, 1)
    w_arrived(False, 4, 0)
    h_pass_on(2)
    w_arrived(False, 4, 1)
    h_pass_on(3)
    w_arrived(True, 3, 0)
    w_arrived(True, 3, 1)
    for j in range(4):
        h_arrival(j, 1).wait_recv()
        h_arrival(j, 2).wait_recv()

    def y_partner(s, i):
        tt = lax.rem(t + 1 + i, NT)
        return remote(pbuf.at[s, tt, 1], rbuf.at[s, 3 + i], y_s.at[s, 3 + i], y_r.at[s, 3 + i], {"dp": xq, "tp": tt})

    def y_own(s, i):
        tt = lax.rem(t + 1 + i, NT)
        return remote(pbuf.at[s, tt, 0], rbuf.at[s, i], y_s.at[s, i], y_r.at[s, i], {"tp": tt})

    for s in range(2):
        def product(i, _):
            tt = lax.rem(t + 1 + i, NT)
            part = jnp.dot(hbuf[s].reshape(2 * TOK, 2 * GW), wbuf[tt], preferred_element_type=F32)
            pbuf[s, tt] = part.astype(BF).reshape(2, TOK, 256)
            y_partner(s, i).start()

            @pl.when(i < NT - 1)
            def _():
                y_own(s, i).start()

            return 0

        lax.fori_loop(0, NT, product, 0)

    def g_copy(s, i):
        return remote(sbuf.at[s, i], gbuf.at[k, 2 * z + s], g_s.at[s, i], g_r.at[s, i], {"ctx": lax.rem(c + i, NC)})

    for s in range(2):
        for i in range(7):
            remote(rbuf.at[s, i], rbuf.at[s, i], y_s.at[s, i], y_r.at[s, i], {"ctx": sib}).wait_recv()
        own = pbuf[s, t, 0].astype(F32)
        for i in range(3):
            own = own + rbuf[s, i].astype(F32)
        red[s, :, 0:256] = own.astype(BF)
        other = rbuf[s, 3].astype(F32)
        for i in range(4, 7):
            other = other + rbuf[s, i].astype(F32)
        red[s, :, 256:512] = other.astype(BF)

        sbuf[s] = jnp.dot(sel[s], red[s], preferred_element_type=F32).astype(BF).reshape(NC, 32, 512)

        def send(i, _):
            g_copy(s, i).start()
            return 0

        lax.fori_loop(1, NC, send, 0)
        gbuf[k, 2 * z + s] = sbuf[s, 0]

    def g_wait(i, _):
        src = lax.rem(c + NC - i, NC)
        for s in range(2):
            place = gbuf.at[lax.rem(src, 2), 2 * (src // 2) + s]
            remote(place, place, g_s.at[s, i], g_r.at[s, i], {"ctx": sib}).wait_recv()
        return 0

    lax.fori_loop(1, NC, g_wait, 0)

    for kk in range(2):
        rows = jnp.dot(take[...], gbuf[kk].reshape(2 * TOK, 512), preferred_element_type=F32).astype(BF)
        first, second = rows[:, :256], rows[:, 256:]
        low = jnp.where(xp == 0, first, second)
        high = jnp.where(xp == 0, second, first)
        for a in range(2):
            at = a * 512 + kk * 256
            out_ref[:, at : at + 128] = low[:, a * 128 : a * 128 + 128]
            out_ref[:, at + 128 : at + 256] = high[:, a * 128 : a * 128 + 128]

    kv_copy(0).wait_send()
    q_copy.wait_send()
    for s in range(1, 5):
        for j in range(2):
            w_copy(False, s, j).wait_send()
            if s < 4:
                w_copy(True, s, j).wait_send()
    for j in range(4):
        h_to_partner(j).wait_send()
        h_to_sibling(j).wait_send()
        h_forward(j).wait_send()
    for s in range(2):
        for i in range(NT):
            y_partner(s, i).wait_send()
            if i < NT - 1:
                y_own(s, i).wait_send()

    def sent(i, _):
        m_copy(i).wait_send()
        g_copy(0, i).wait_send()
        g_copy(1, i).wait_send()
        return 0

    lax.fori_loop(1, NC, sent, 0)


def local(queries, key_value_vectors, out_weight, doc_lengths, shard_of):
    owner = shard_of.reshape(NC, 16)[:, 0]
    block = jnp.arange(NC, dtype=jnp.int32)
    hit = owner[:, None] == block[None, :]
    first = jnp.min(jnp.where(hit, block[:, None], NC - 1), axis=0)
    second = jnp.max(jnp.where(hit, block[:, None], 0), axis=0)
    sends = jnp.max(hit.astype(jnp.int32), axis=0)
    row = jnp.concatenate([first, second, sends, jnp.zeros((128 - 3 * NC,), jnp.int32)])
    meta = jnp.broadcast_to(row[None, :], (8, 128))
    dma = pltpu.SemaphoreType.DMA
    return pl.pallas_call(
        kernel,
        out_shape=jax.ShapeDtypeStruct((TOK, 1024), BF),
        in_specs=[pl.BlockSpec(memory_space=pl.ANY)] * 4 + [pl.BlockSpec(memory_space=pltpu.SMEM)],
        out_specs=pl.BlockSpec(memory_space=pltpu.VMEM),
        scratch_shapes=[
            pltpu.VMEM((2, TOK, GW), BF),
            pltpu.VMEM((6, TOK, 256), BF),
            pltpu.VMEM((6, TOK, 256), BF),
            pltpu.VMEM((2, TOK, NK), F32),
            pltpu.VMEM((2, 2, TOK, 2 * GW), BF),
            pltpu.VMEM((NT, 2 * GW, 256), BF),
            pltpu.VMEM((2, NT, 2, TOK, 256), BF),
            pltpu.VMEM((2, 7, TOK, 256), BF),
            pltpu.VMEM((2, TOK, 512), BF),
            pltpu.VMEM((2, NC, 32, 512), BF),
            pltpu.VMEM((2, NC, 32, 512), BF),
            pltpu.VMEM((2, 512, TOK), BF),
            pltpu.VMEM((TOK, 512), BF),
            pltpu.VMEM((NC, 8, 128), jnp.int32),
            pltpu.SMEM((NC, 8, 128), jnp.int32),
            dma((5,)),
            dma((NC,)), dma((NC,)),
            dma((1,)), dma((1,)),
            dma((5,)), dma((6,)),
            dma((14,)), dma((14,)),
            dma((3, 4)), dma((3, 4)),
            dma((2, 7)), dma((2, 7)),
            dma((2, NC)), dma((2, NC)),
        ],
        compiler_params=pltpu.CompilerParams(
            collective_id=0, has_side_effects=True, vmem_limit_bytes=56 * 1024 * 1024
        ),
        cost_estimate=pl.CostEstimate(flops=7_000_000_000, bytes_accessed=4_000_000, transcendentals=5_000_000),
    )(queries, key_value_vectors, out_weight, meta, doc_lengths)


def solution(mesh):
    placed = (
        P(("dp", "ctx"), "tp"),
        P(("dp", "ctx"), "tp"),
        P("tp", "ctx"),
        P("dp"),
        P(("dp", "ctx")),
    )
    return jax.shard_map(
        local, mesh=mesh, in_specs=placed, out_specs=P(("dp", "ctx"), "tp"), check_vma=False
    )
```

```python
import math

import jax
import jax.numpy as jnp
from jax import lax
from jax.experimental import pallas as pl
from jax.experimental.pallas import tpu as pltpu
from jax.sharding import PartitionSpec as P

MESH = pl.DeviceIdType.MESH
BF = jnp.bfloat16
F32 = jnp.float32
HS = 128
TOK = 256
GH = 8
GW = GH * HS
NK = 5 * TOK
SCALE = math.log2(math.e) / math.sqrt(HS)
NZ = 8
NC = 16
NT = 4
UP, DOWN = 2, 5
SHARED = 768
BOTH = 2 * GW - 2 * SHARED


def mult(value, of):
    return pl.multiple_of(value, of)


def kernel(
    q_ref, kv_ref, w_ref, meta_ref, len_ref, out_ref,
    qbuf, kvb, vo, bias, hbuf, wbuf, pbuf, rbuf, red, sbuf, gbuf, sel, take, mbuf, msm,
    loc, m_s, m_r, q_s, q_r, kv_s, kv_r, w_s, w_r, h_s, h_r, y_s, y_r, g_s, g_r,
):
    x = lax.axis_index("dp")
    c = lax.axis_index("ctx")
    t = lax.axis_index("tp")
    z = c // 2
    k = lax.rem(c, 2)
    xp = lax.rem(x, 2)
    xq = x + 1 - 2 * xp
    sib = c + 1 - 2 * k
    xs = 3 - x
    half = lax.rem(x + x // 2, 2)
    upper = x // 2

    def remote(src, dst, send, recv, where):
        return pltpu.make_async_remote_copy(
            src_ref=src, dst_ref=dst, send_sem=send, recv_sem=recv, device_id=where, device_id_type=MESH
        )

    barrier = pltpu.get_barrier_semaphore()

    def greet_ctx(i, _):
        pl.semaphore_signal(barrier, inc=1, device_id={"ctx": lax.rem(c + i, NC)}, device_id_type=MESH)
        return 0

    lax.fori_loop(1, NC, greet_ctx, 0)
    for i in range(1, NT):
        pl.semaphore_signal(barrier, inc=1, device_id={"tp": lax.rem(t + i, NT)}, device_id_type=MESH)
    for i in range(NT):
        pl.semaphore_signal(barrier, inc=1, device_id={"dp": xq, "tp": lax.rem(t + i, NT)}, device_id_type=MESH)
    pl.semaphore_signal(barrier, inc=1, device_id={"dp": xs}, device_id_type=MESH)
    pl.semaphore_wait(barrier, NC - 1 + NT - 1 + NT + 1)

    def kv_copy(i):
        if i == 0:
            g, slot, to = 1 - k, 4 + k, sib
        else:
            hop, g = (i + 1) // 2, (i + 1) % 2
            slot, to = 4 - 2 * hop + k, 2 * lax.rem(z + hop, NZ) + g
        return remote(
            kv_ref.at[:, pl.ds(mult(g * 256, 256), 256)], kvb.at[slot], kv_s.at[i], kv_r.at[slot], {"ctx": to}
        )

    def kv_arrival(slot):
        return remote(kvb.at[slot], kvb.at[slot], kv_s.at[0], kv_r.at[slot], {"ctx": sib})

    q_copy = remote(
        q_ref.at[:, pl.ds(mult((1 - k) * GW, GW), GW)], qbuf.at[k], q_s.at[0], q_r.at[0], {"ctx": sib}
    )
    q_arrival = remote(qbuf.at[1 - k], qbuf.at[1 - k], q_s.at[0], q_r.at[0], {"ctx": sib})

    def w_rows(j, mine=True):
        if j == 0:
            return pl.ds(mult((upper if mine else 1 - upper) * SHARED, SHARED), SHARED)
        return pl.ds(2 * SHARED, BOTH)

    def w_place(zz, rows):
        return wbuf.at[zz // 2, rows, pl.ds(mult(lax.rem(zz, 2) * 128, 128), 128)]

    def w_block(up, s):
        return lax.rem(z + (NZ - s if up else s), NZ)

    def w_index(up, s):
        return (0 if up else UP) + s - 1

    def w_copy(up, s, j):
        zz = w_block(up, s - 1)
        to = 2 * lax.rem(z + (1 if up else NZ - 1), NZ) + k
        n = w_index(up, s)
        place = w_place(zz, w_rows(j))
        src = w_ref.at[w_rows(j), pl.ds(mult(half * 128, 128), 128)] if s == 1 else place
        return remote(src, place, w_s.at[n, j], w_r.at[n, j], {"ctx": to})

    def w_share(up, s):
        n = w_index(up, s)
        place = w_place(w_block(up, s), w_rows(0))
        return remote(place, place, w_s.at[n, 2], w_r.at[n, 2], {"dp": xs})

    def w_shared(up, s):
        n = w_index(up, s)
        place = w_place(w_block(up, s), w_rows(0, False))
        return remote(place, place, w_s.at[n, 2], w_r.at[n, 2], {"dp": xs})

    def w_arrived(up, s):
        n = w_index(up, s)
        for j in range(2):
            place = w_place(w_block(up, s), w_rows(j))
            remote(place, place, w_s.at[n, j], w_r.at[n, j], {"ctx": sib}).wait_recv()
            if s < (UP if up else DOWN):
                w_copy(up, s + 1, j).start()
            if j == 0:
                w_share(up, s).start()

    w_steps = [(True, s) for s in range(1, UP + 1)] + [(False, s) for s in range(1, DOWN + 1)]

    local_copies = [
        pltpu.make_async_copy(q_ref.at[:, pl.ds(mult(k * GW, GW), GW)], qbuf.at[k], loc.at[0]),
        pltpu.make_async_copy(kv_ref.at[:, pl.ds(mult(k * 256, 256), 256)], kvb.at[4 + k], loc.at[1]),
        pltpu.make_async_copy(w_ref.at[:, pl.ds(mult(half * 128, 128), 128)],
                              wbuf.at[z // 2, :, pl.ds(mult(lax.rem(z, 2) * 128, 128), 128)], loc.at[2]),
        pltpu.make_async_copy(meta_ref, mbuf.at[c], loc.at[3]),
    ]

    def m_copy(i):
        return remote(meta_ref, mbuf.at[c], m_s.at[i], m_r.at[i], {"ctx": lax.rem(c + i, NC)})

    for i in (1, 2, 0):
        kv_copy(i).start()

    @pl.when(k == 1)
    def _():
        kv_copy(3).start()
        kv_copy(4).start()

    w_copy(False, 1, 0).start()
    w_copy(False, 1, 1).start()
    q_copy.start()
    for copy in local_copies:
        copy.start()

    def m_send(i, _):
        m_copy(i).start()
        return 0

    lax.fori_loop(1, NC, m_send, 0)

    ends = []
    total = jnp.int32(0)
    for d in range(8):
        total = total + len_ref[d]
        ends.append(total)
    for s in range(2):
        base = z * 512 + s * 256
        rows = lax.broadcasted_iota(jnp.int32, (TOK, 1), 0)
        start = jnp.zeros((TOK, 1), jnp.int32)
        for e in ends:
            start = jnp.where(rows + base >= e, e, start)
        keys = lax.broadcasted_iota(jnp.int32, (TOK, NK), 1)
        seen = (keys <= rows + 1024) & (keys >= start - (base - 1024))
        bias[s] = jnp.where(seen, 0.0, -1e30).astype(F32)

    kv_arrival(2).wait_recv()
    kv_arrival(3).wait_recv()

    @pl.when(k == 0)
    def _():
        kv_copy(3).start()
        kv_copy(4).start()

    for copy in local_copies:
        copy.wait()
    q_arrival.wait_recv()
    kv_arrival(5 - k).wait_recv()
    w_arrived(False, 1)

    def widen(slot, count):
        vo[slot : slot + count, :, 0:HS] = kvb[slot : slot + count, :, HS:]
        vo[slot : slot + count, :, HS:] = jnp.ones((count, TOK, HS), BF)

    widen(2, 4)
    kv_arrival(1).wait_recv()
    widen(1, 1)

    def h_lanes(j, kk):
        return pl.ds(mult(kk * GW + j * 256, 256), 256)

    def h_to_partner(s, j):
        return remote(hbuf.at[s, 0, :, h_lanes(j, k)], hbuf.at[s, 1, :, h_lanes(j, k)],
                      h_s.at[0, s, j], h_r.at[0, s, j], {"dp": xq})

    def h_to_sibling(s, j):
        place = hbuf.at[s, 0, :, h_lanes(j, k)]
        return remote(place, place, h_s.at[1, s, j], h_r.at[1, s, j], {"ctx": sib})

    def h_forward(s, j):
        place = hbuf.at[s, 1, :, h_lanes(j, k)]
        return remote(place, place, h_s.at[2, s, j], h_r.at[2, s, j], {"ctx": sib})

    def h_arrival(s, j, way):
        place = hbuf.at[s, 1, :, h_lanes(j, k)] if way == 0 else hbuf.at[s, way - 1, :, h_lanes(j, 1 - k)]
        return remote(place, place, h_s.at[way, s, j], h_r.at[way, s, j], {"ctx": sib})

    def attend(s, j):
        keys = kvb[s : s + 5, :, 0:HS].reshape(NK, HS)
        values = vo[s : s + 5].reshape(NK, 2 * HS)
        heads = (2 * j, 2 * j + 1)
        scores = [
            lax.dot_general(qbuf[s, :, h * HS : (h + 1) * HS], keys, (((1,), (1,)), ((), ())),
                            preferred_element_type=F32)
            for h in heads
        ]
        for h, score in zip(heads, scores):
            score = score * SCALE + bias[s]
            weights = jnp.exp2(score - jnp.max(score, axis=1, keepdims=True)).astype(BF)
            mixed = jnp.dot(weights, values, preferred_element_type=F32)
            hbuf[s, 0, :, pl.ds(mult(k * GW + h * HS, HS), HS)] = (mixed[:, :HS] / mixed[:, HS:]).astype(BF)
        h_to_partner(s, j).start()
        h_to_sibling(s, j).start()

    def h_pass_on(s, j):
        h_arrival(s, j, 0).wait_recv()
        h_forward(s, j).start()

    attend(1, 0)
    w_arrived(False, 2)
    attend(1, 1)
    attend(1, 2)
    attend(1, 3)
    for i in (1, 2, 3, 4):
        kv_copy(i).wait_send()
    w_copy(True, 1, 0).start()
    w_copy(True, 1, 1).start()
    kv_arrival(0).wait_recv()
    widen(0, 1)
    attend(0, 0)
    h_pass_on(1, 0)
    w_arrived(False, 3)
    attend(0, 1)
    h_pass_on(1, 1)
    attend(0, 2)
    h_pass_on(1, 2)
    w_arrived(True, 1)
    attend(0, 3)
    h_pass_on(1, 3)
    w_arrived(False, 4)

    def m_wait(i, _):
        src = lax.rem(c + NC - i, NC)
        remote(mbuf.at[src], mbuf.at[src], m_s.at[i], m_r.at[i], {"ctx": sib}).wait_recv()
        return 0

    lax.fori_loop(1, NC, m_wait, 0)
    table = pltpu.make_async_copy(mbuf, msm, loc.at[4])
    table.start()
    table.wait()

    def owner(n, b):
        return msm[n, b // 8, (b % 8) * 16]

    lane = lax.broadcasted_iota(jnp.int32, (1, TOK), 1)
    for s in range(2):
        owners = [owner(2 * z + s, b) for b in range(16)]
        wanted = jnp.zeros((1, TOK), jnp.int32)
        for b in range(16):
            second = jnp.int32(0)
            for e in range(b):
                second = second + jnp.where(owners[e] == owners[b], 16, 0)
            slot = owners[b] - c
            slot = jnp.where(slot < 0, slot + NC, slot)
            wanted = jnp.where(lane // 16 == b, slot * 32 + second, wanted)
        wanted = wanted + lax.rem(lane, 16)
        row = lax.broadcasted_iota(jnp.int32, (512, TOK), 0)
        sel[s] = jnp.where(row == wanted, 1.0, 0.0).astype(BF)

    counts = []
    count = jnp.int32(0)
    for n in range(NC):
        any_block = jnp.int32(0)
        for b in range(16):
            any_block = jnp.maximum(any_block, jnp.where(owner(n, b) == c, 1, 0))
        count = count + any_block
        counts.append(count)

    def place(r, _):
        src = jnp.int32(0)
        for n in range(NC - 1):
            src = src + jnp.where(counts[n] <= r, 1, 0)
        row = lax.broadcasted_iota(jnp.int32, (32, 512), 0)
        column = lax.broadcasted_iota(jnp.int32, (32, 512), 1)
        take[pl.ds(mult(r * 32, 32), 32), :] = jnp.where(column == row + src * 32, 1.0, 0.0).astype(BF)
        return 0

    lax.fori_loop(0, 8, place, 0)

    h_pass_on(0, 0)
    h_pass_on(0, 1)
    w_arrived(True, 2)
    h_pass_on(0, 2)
    w_arrived(False, 5)
    h_pass_on(0, 3)
    for up, s in w_steps:
        w_shared(up, s).wait_recv()
    for s in range(2):
        for j in range(4):
            h_arrival(s, j, 1).wait_recv()
            h_arrival(s, j, 2).wait_recv()

    def y_partner(s, i):
        tt = lax.rem(t + 1 + i, NT)
        return remote(pbuf.at[s, tt, 1], rbuf.at[s, 3 + i], y_s.at[s, 3 + i], y_r.at[s, 3 + i], {"dp": xq, "tp": tt})

    def y_own(s, i):
        tt = lax.rem(t + 1 + i, NT)
        return remote(pbuf.at[s, tt, 0], rbuf.at[s, i], y_s.at[s, i], y_r.at[s, i], {"tp": tt})

    for s in range(2):
        def product(i, _):
            tt = lax.rem(t + 1 + i, NT)
            part = jnp.dot(hbuf[s].reshape(2 * TOK, 2 * GW), wbuf[tt], preferred_element_type=F32)
            pbuf[s, tt] = part.astype(BF).reshape(2, TOK, 256)
            y_partner(s, i).start()

            @pl.when(i < NT - 1)
            def _():
                y_own(s, i).start()

            return 0

        lax.fori_loop(0, NT, product, 0)

    def g_copy(s, i):
        return remote(sbuf.at[s, i], gbuf.at[k, 2 * z + s], g_s.at[s, i], g_r.at[s, i], {"ctx": lax.rem(c + i, NC)})

    for s in range(2):
        for i in range(7):
            remote(rbuf.at[s, i], rbuf.at[s, i], y_s.at[s, i], y_r.at[s, i], {"ctx": sib}).wait_recv()
        own = pbuf[s, t, 0].astype(F32)
        for i in range(3):
            own = own + rbuf[s, i].astype(F32)
        red[s, :, 0:256] = own.astype(BF)
        other = rbuf[s, 3].astype(F32)
        for i in range(4, 7):
            other = other + rbuf[s, i].astype(F32)
        red[s, :, 256:512] = other.astype(BF)

        sbuf[s] = jnp.dot(sel[s], red[s], preferred_element_type=F32).astype(BF).reshape(NC, 32, 512)

        def send(i, _):
            g_copy(s, i).start()
            return 0

        lax.fori_loop(1, NC, send, 0)
        gbuf[k, 2 * z + s] = sbuf[s, 0]

    def g_wait(i, _):
        src = lax.rem(c + NC - i, NC)
        for s in range(2):
            place = gbuf.at[lax.rem(src, 2), 2 * (src // 2) + s]
            remote(place, place, g_s.at[s, i], g_r.at[s, i], {"ctx": sib}).wait_recv()
        return 0

    lax.fori_loop(1, NC, g_wait, 0)

    for kk in range(2):
        rows = jnp.dot(take[...], gbuf[kk].reshape(2 * TOK, 512), preferred_element_type=F32).astype(BF)
        first, second = rows[:, :256], rows[:, 256:]
        low = jnp.where(half == 0, first, second)
        high = jnp.where(half == 0, second, first)
        for a in range(2):
            at = a * 512 + kk * 256
            out_ref[:, at : at + 128] = low[:, a * 128 : a * 128 + 128]
            out_ref[:, at + 128 : at + 256] = high[:, a * 128 : a * 128 + 128]

    kv_copy(0).wait_send()
    q_copy.wait_send()
    for up, s in w_steps:
        w_copy(up, s, 0).wait_send()
        w_copy(up, s, 1).wait_send()
        w_share(up, s).wait_send()
    for s in range(2):
        for j in range(4):
            h_to_partner(s, j).wait_send()
            h_to_sibling(s, j).wait_send()
            h_forward(s, j).wait_send()
    for s in range(2):
        for i in range(NT):
            y_partner(s, i).wait_send()
            if i < NT - 1:
                y_own(s, i).wait_send()

    def sent(i, _):
        m_copy(i).wait_send()
        g_copy(0, i).wait_send()
        g_copy(1, i).wait_send()
        return 0

    lax.fori_loop(1, NC, sent, 0)


def local(queries, key_value_vectors, out_weight, doc_lengths, shard_of):
    meta = shard_of.reshape(2, 128)
    dma = pltpu.SemaphoreType.DMA
    return pl.pallas_call(
        kernel,
        out_shape=jax.ShapeDtypeStruct((TOK, 1024), BF),
        in_specs=[pl.BlockSpec(memory_space=pl.ANY)] * 4 + [pl.BlockSpec(memory_space=pltpu.SMEM)],
        out_specs=pl.BlockSpec(memory_space=pltpu.VMEM),
        scratch_shapes=[
            pltpu.VMEM((2, TOK, GW), BF),
            pltpu.VMEM((6, TOK, 256), BF),
            pltpu.VMEM((6, TOK, 256), BF),
            pltpu.VMEM((2, TOK, NK), F32),
            pltpu.VMEM((2, 2, TOK, 2 * GW), BF),
            pltpu.VMEM((NT, 2 * GW, 256), BF),
            pltpu.VMEM((2, NT, 2, TOK, 256), BF),
            pltpu.VMEM((2, 7, TOK, 256), BF),
            pltpu.VMEM((2, TOK, 512), BF),
            pltpu.VMEM((2, NC, 32, 512), BF),
            pltpu.VMEM((2, NC, 32, 512), BF),
            pltpu.VMEM((2, 512, TOK), BF),
            pltpu.VMEM((TOK, 512), BF),
            pltpu.VMEM((NC, 2, 128), jnp.int32),
            pltpu.SMEM((NC, 2, 128), jnp.int32),
            dma((5,)),
            dma((NC,)), dma((NC,)),
            dma((1,)), dma((1,)),
            dma((5,)), dma((6,)),
            dma((7, 3)), dma((7, 3)),
            dma((3, 2, 4)), dma((3, 2, 4)),
            dma((2, 7)), dma((2, 7)),
            dma((2, NC)), dma((2, NC)),
        ],
        compiler_params=pltpu.CompilerParams(
            collective_id=0, has_side_effects=True, vmem_limit_bytes=56 * 1024 * 1024
        ),
        cost_estimate=pl.CostEstimate(flops=7_000_000_000, bytes_accessed=4_000_000, transcendentals=5_000_000),
    )(queries, key_value_vectors, out_weight, meta, doc_lengths)


def solution(mesh):
    placed = (
        P(("dp", "ctx"), "tp"),
        P(("dp", "ctx"), "tp"),
        P("tp", "ctx"),
        P("dp"),
        P(("dp", "ctx")),
    )
    return jax.shard_map(
        local, mesh=mesh, in_specs=placed, out_specs=P(("dp", "ctx"), "tp"), check_vma=False
    )
```

```python
import math

import jax
import jax.numpy as jnp
from jax import lax
from jax.experimental import pallas as pl
from jax.experimental.pallas import tpu as pltpu
from jax.sharding import PartitionSpec as P

MESH = pl.DeviceIdType.MESH
BF = jnp.bfloat16
F32 = jnp.float32
HS = 128
TOK = 256
GH = 8
GW = GH * HS
NK = 5 * TOK
SCALE = math.log2(math.e) / math.sqrt(HS)
NZ = 8
NC = 16
NT = 4
UP, DOWN = 3, 5
SHARED = 704
BOTH = 2 * GW - 2 * SHARED


def mult(value, of):
    return pl.multiple_of(value, of)


def kernel(
    q_ref, kv_ref, w_ref, meta_ref, len_ref, out_ref,
    qbuf, kvb, vo, bias, hbuf, wbuf, pbuf, rbuf, sbuf, gbuf, sel, take, mbuf, msm,
    loc, m_s, m_r, q_s, q_r, kv_s, kv_r, w_s, w_r, h_s, h_r, y_s, y_r, g_s, g_r,
):
    x = lax.axis_index("dp")
    c = lax.axis_index("ctx")
    t = lax.axis_index("tp")
    z = c // 2
    k = lax.rem(c, 2)
    xp = lax.rem(x, 2)
    xq = x + 1 - 2 * xp
    sib = c + 1 - 2 * k
    xs = 3 - x
    half = lax.rem(x + x // 2, 2)
    upper = x // 2

    def remote(src, dst, send, recv, where):
        return pltpu.make_async_remote_copy(
            src_ref=src, dst_ref=dst, send_sem=send, recv_sem=recv, device_id=where, device_id_type=MESH
        )

    barrier = pltpu.get_barrier_semaphore()

    def greet_ctx(i, _):
        pl.semaphore_signal(barrier, inc=1, device_id={"ctx": lax.rem(c + i, NC)}, device_id_type=MESH)
        return 0

    lax.fori_loop(1, NC, greet_ctx, 0)
    for i in range(1, NT):
        pl.semaphore_signal(barrier, inc=1, device_id={"tp": lax.rem(t + i, NT)}, device_id_type=MESH)
    for i in range(NT):
        pl.semaphore_signal(barrier, inc=1, device_id={"dp": xq, "tp": lax.rem(t + i, NT)}, device_id_type=MESH)
    pl.semaphore_signal(barrier, inc=1, device_id={"dp": xs}, device_id_type=MESH)
    pl.semaphore_wait(barrier, NC - 1 + NT - 1 + NT + 1)

    def kv_copy(i):
        if i == 0:
            g, slot, to = 1 - k, 4 + k, sib
        else:
            hop, g = (i + 1) // 2, (i + 1) % 2
            slot, to = 4 - 2 * hop + k, 2 * lax.rem(z + hop, NZ) + g
        return remote(
            kv_ref.at[:, pl.ds(mult(g * 256, 256), 256)], kvb.at[slot], kv_s.at[i], kv_r.at[slot], {"ctx": to}
        )

    def kv_arrival(slot):
        return remote(kvb.at[slot], kvb.at[slot], kv_s.at[0], kv_r.at[slot], {"ctx": sib})

    q_copy = remote(
        q_ref.at[:, pl.ds(mult((1 - k) * GW, GW), GW)], qbuf.at[k], q_s.at[0], q_r.at[0], {"ctx": sib}
    )
    q_arrival = remote(qbuf.at[1 - k], qbuf.at[1 - k], q_s.at[0], q_r.at[0], {"ctx": sib})

    def w_rows(j, mine=True):
        if j == 0:
            return pl.ds(mult((upper if mine else 1 - upper) * SHARED, 16), SHARED)
        return pl.ds(2 * SHARED, BOTH)

    def w_place(zz, rows):
        return wbuf.at[zz // 2, rows, pl.ds(mult(lax.rem(zz, 2) * 128, 128), 128)]

    def w_block(up, s):
        return lax.rem(z + (NZ - s if up else s), NZ)

    def w_index(up, s):
        return (0 if up else UP) + s - 1

    def w_copy(up, s, j):
        zz = w_block(up, s - 1)
        to = 2 * lax.rem(z + (1 if up else NZ - 1), NZ) + k
        n = w_index(up, s)
        place = w_place(zz, w_rows(j))
        src = w_ref.at[w_rows(j), pl.ds(mult(half * 128, 128), 128)] if s == 1 else place
        return remote(src, place, w_s.at[n, j], w_r.at[n, j], {"ctx": to})

    def w_share(up, s):
        n = w_index(up, s)
        place = w_place(w_block(up, s), w_rows(0))
        return remote(place, place, w_s.at[n, 2], w_r.at[n, 2], {"dp": xs})

    def w_shared(up, s):
        n = w_index(up, s)
        place = w_place(w_block(up, s), w_rows(0, False))
        return remote(place, place, w_s.at[n, 2], w_r.at[n, 2], {"dp": xs})

    def w_parts(up, s):
        return (1,) if up and s == UP else (0,) if not up and s == DOWN else (0, 1)

    def w_start(up, s, j):
        if s <= (UP if up else DOWN) and j in w_parts(up, s):
            w_copy(up, s, j).start()

    def w_arrived(up, s, j):
        n = w_index(up, s)
        place = w_place(w_block(up, s), w_rows(j))
        remote(place, place, w_s.at[n, j], w_r.at[n, j], {"ctx": sib}).wait_recv()
        w_start(up, s + 1, j)
        if j == 0:
            w_share(up, s).start()

    w_steps = [(True, s) for s in range(1, UP + 1)] + [(False, s) for s in range(1, DOWN + 1)]

    local_copies = [
        pltpu.make_async_copy(q_ref.at[:, pl.ds(mult(k * GW, GW), GW)], qbuf.at[k], loc.at[0]),
        pltpu.make_async_copy(kv_ref.at[:, pl.ds(mult(k * 256, 256), 256)], kvb.at[4 + k], loc.at[1]),
        pltpu.make_async_copy(w_ref.at[:, pl.ds(mult(half * 128, 128), 128)],
                              wbuf.at[z // 2, :, pl.ds(mult(lax.rem(z, 2) * 128, 128), 128)], loc.at[2]),
        pltpu.make_async_copy(meta_ref, mbuf.at[c], loc.at[3]),
    ]

    def m_copy(i):
        return remote(meta_ref, mbuf.at[c], m_s.at[i], m_r.at[i], {"ctx": lax.rem(c + i, NC)})

    kv_copy(0).start()
    w_copy(False, 1, 0).start()
    kv_copy(1).start()
    kv_copy(2).start()

    @pl.when(k == 1)
    def _():
        kv_copy(3).start()
        kv_copy(4).start()
        w_copy(True, 1, 0).start()

    @pl.when(k == 0)
    def _():
        w_copy(True, 1, 0).start()
        kv_copy(3).start()
        kv_copy(4).start()

    w_copy(False, 1, 1).start()
    w_copy(True, 1, 1).start()
    q_copy.start()
    for copy in local_copies:
        copy.start()

    def m_send(i, _):
        m_copy(i).start()
        return 0

    lax.fori_loop(1, NC, m_send, 0)

    ends = []
    total = jnp.int32(0)
    for d in range(8):
        total = total + len_ref[d]
        ends.append(total)
    for s in range(2):
        base = z * 512 + s * 256
        rows = lax.broadcasted_iota(jnp.int32, (TOK, 1), 0)
        start = jnp.zeros((TOK, 1), jnp.int32)
        for e in ends:
            start = jnp.where(rows + base >= e, e, start)
        keys = lax.broadcasted_iota(jnp.int32, (TOK, NK), 1)
        seen = (keys <= rows + 1024) & (keys >= start - (base - 1024))
        bias[s] = jnp.where(seen, 0.0, -1e30).astype(F32)

    kv_arrival(2).wait_recv()
    kv_arrival(3).wait_recv()

    for copy in local_copies:
        copy.wait()
    q_arrival.wait_recv()
    kv_arrival(5 - k).wait_recv()
    def widen(slot, count):
        vo[slot : slot + count, :, 0:HS] = kvb[slot : slot + count, :, HS:]
        vo[slot : slot + count, :, HS:] = jnp.ones((count, TOK, HS), BF)

    widen(2, 4)
    w_arrived(False, 1, 0)
    w_arrived(False, 1, 1)
    w_arrived(False, 2, 0)
    kv_arrival(1).wait_recv()
    widen(1, 1)

    def h_lanes(j, kk):
        return pl.ds(mult(kk * GW + j * 256, 256), 256)

    def h_to_partner(s, j):
        return remote(hbuf.at[s, 0, :, h_lanes(j, k)], hbuf.at[s, 1, :, h_lanes(j, k)],
                      h_s.at[0, s, j], h_r.at[0, s, j], {"dp": xq})

    def h_to_sibling(s, j):
        place = hbuf.at[s, 0, :, h_lanes(j, k)]
        return remote(place, place, h_s.at[1, s, j], h_r.at[1, s, j], {"ctx": sib})

    def h_forward(s, j):
        place = hbuf.at[s, 1, :, h_lanes(j, k)]
        return remote(place, place, h_s.at[2, s, j], h_r.at[2, s, j], {"ctx": sib})

    def h_arrival(s, j, way):
        place = hbuf.at[s, 1, :, h_lanes(j, k)] if way == 0 else hbuf.at[s, way - 1, :, h_lanes(j, 1 - k)]
        return remote(place, place, h_s.at[way, s, j], h_r.at[way, s, j], {"ctx": sib})

    def attend(s, j):
        keys = kvb[s : s + 5, :, 0:HS].reshape(NK, HS)
        values = vo[s : s + 5].reshape(NK, 2 * HS)
        heads = (2 * j, 2 * j + 1)
        scores = [
            lax.dot_general(qbuf[s, :, h * HS : (h + 1) * HS], keys, (((1,), (1,)), ((), ())),
                            preferred_element_type=F32)
            for h in heads
        ]
        for h, score in zip(heads, scores):
            score = score * SCALE + bias[s]
            weights = jnp.exp2(score - jnp.max(score, axis=1, keepdims=True)).astype(BF)
            mixed = jnp.dot(weights, values, preferred_element_type=F32)
            hbuf[s, 0, :, pl.ds(mult(k * GW + h * HS, HS), HS)] = (mixed[:, :HS] / mixed[:, HS:]).astype(BF)
        h_to_partner(s, j).start()
        h_to_sibling(s, j).start()

    def h_pass_on(s, j):
        h_arrival(s, j, 0).wait_recv()
        h_forward(s, j).start()

    attend(1, 0)
    w_arrived(False, 2, 1)
    attend(1, 1)
    w_arrived(True, 1, 0)
    attend(1, 2)
    attend(1, 3)
    w_arrived(False, 3, 0)
    kv_arrival(0).wait_recv()
    widen(0, 1)
    attend(0, 0)
    h_pass_on(1, 0)
    w_arrived(True, 1, 1)
    w_arrived(False, 3, 1)
    attend(0, 1)
    h_pass_on(1, 1)
    attend(0, 2)
    h_pass_on(1, 2)
    w_arrived(True, 2, 0)
    w_arrived(False, 4, 0)
    attend(0, 3)
    h_pass_on(1, 3)

    def m_wait(i, _):
        src = lax.rem(c + NC - i, NC)
        remote(mbuf.at[src], mbuf.at[src], m_s.at[i], m_r.at[i], {"ctx": sib}).wait_recv()
        return 0

    lax.fori_loop(1, NC, m_wait, 0)
    table = pltpu.make_async_copy(mbuf, msm, loc.at[4])
    table.start()
    table.wait()

    def owner(n, b):
        return msm[n, b // 8, (b % 8) * 16]

    lane = lax.broadcasted_iota(jnp.int32, (1, TOK), 1)
    for s in range(2):
        owners = [owner(2 * z + s, b) for b in range(16)]
        wanted = jnp.zeros((1, TOK), jnp.int32)
        for b in range(16):
            second = jnp.int32(0)
            for e in range(b):
                second = second + jnp.where(owners[e] == owners[b], 16, 0)
            slot = owners[b] - c
            slot = jnp.where(slot < 0, slot + NC, slot)
            wanted = jnp.where(lane // 16 == b, slot * 32 + second, wanted)
        wanted = wanted + lax.rem(lane, 16)
        row = lax.broadcasted_iota(jnp.int32, (512, TOK), 0)
        sel[s] = jnp.where(row == wanted, 1.0, 0.0).astype(BF)

    counts = []
    count = jnp.int32(0)
    for n in range(NC):
        any_block = jnp.int32(0)
        for b in range(16):
            any_block = jnp.maximum(any_block, jnp.where(owner(n, b) == c, 1, 0))
        count = count + any_block
        counts.append(count)

    def place(r, _):
        src = jnp.int32(0)
        for n in range(NC - 1):
            src = src + jnp.where(counts[n] <= r, 1, 0)
        row = lax.broadcasted_iota(jnp.int32, (32, 512), 0)
        column = lax.broadcasted_iota(jnp.int32, (32, 512), 1)
        take[pl.ds(mult(r * 32, 32), 32), :] = jnp.where(column == row + src * 32, 1.0, 0.0).astype(BF)
        return 0

    lax.fori_loop(0, 8, place, 0)

    w_arrived(False, 4, 1)
    w_arrived(True, 2, 1)
    h_pass_on(0, 0)
    h_pass_on(0, 1)
    w_arrived(False, 5, 0)
    w_arrived(True, 3, 1)
    h_pass_on(0, 2)
    h_pass_on(0, 3)
    for up, s in w_steps:
        if 0 in w_parts(up, s):
            w_shared(up, s).wait_recv()
    for s in range(2):
        for j in range(4):
            h_arrival(s, j, 1).wait_recv()
            h_arrival(s, j, 2).wait_recv()

    def y_copy(s, a, i):
        own = i < NT - 1
        tt = lax.rem(t + 1 + (i if own else i - NT + 1), NT)
        where = {"tp": tt} if own else {"dp": xq, "tp": tt}
        return remote(pbuf.at[s, tt, a, 0 if own else 1], rbuf.at[s, a, i], y_s.at[s, a, i], y_r.at[s, a, i], where)

    for s in range(2):
        for i in range(NT):
            tt = lax.rem(t + 1 + i, NT)
            part = jnp.dot(hbuf[s].reshape(2 * TOK, 2 * GW), wbuf[tt], preferred_element_type=F32).astype(BF)
            for a in range(2):
                pbuf[s, tt, a] = part[:, a * 128 : a * 128 + 128].reshape(2, TOK, 128)
            y_copy(s, 0, NT - 1 + i).start()
            if i < NT - 1:
                y_copy(s, 0, i).start()
        for i in range(NT):
            y_copy(s, 1, NT - 1 + i).start()
            if i < NT - 1:
                y_copy(s, 1, i).start()

    def g_copy(s, e, i):
        return remote(sbuf.at[s, e, i], gbuf.at[k, e, 2 * z + s], g_s.at[s, e, i], g_r.at[s, e, i],
                      {"ctx": lax.rem(c + i, NC)})

    for s in range(2):
        for e in range(2):
            for i in range(7):
                place = rbuf.at[s, e, i]
                remote(place, place, y_s.at[s, e, i], y_r.at[s, e, i], {"ctx": sib}).wait_recv()
            own = pbuf[s, t, e, 0].astype(F32)
            for i in range(3):
                own = own + rbuf[s, e, i].astype(F32)
            other = rbuf[s, e, 3].astype(F32)
            for i in range(4, 7):
                other = other + rbuf[s, e, i].astype(F32)
            both = jnp.concatenate([own.astype(BF), other.astype(BF)], axis=1)
            rows = jnp.dot(sel[s], both, preferred_element_type=F32)
            sbuf[s, e] = rows.astype(BF).reshape(NC, 32, 256)

            def send(i, _):
                g_copy(s, e, i).start()
                return 0

            lax.fori_loop(1, NC, send, 0)
            gbuf[k, e, 2 * z + s] = sbuf[s, e, 0]

    def g_wait(i, _):
        src = lax.rem(c + NC - i, NC)
        for s in range(2):
            for e in range(2):
                place = gbuf.at[lax.rem(src, 2), e, 2 * (src // 2) + s]
                remote(place, place, g_s.at[s, e, i], g_r.at[s, e, i], {"ctx": sib}).wait_recv()
        return 0

    lax.fori_loop(1, NC, g_wait, 0)

    for kk in range(2):
        for a in range(2):
            rows = jnp.dot(take[...], gbuf[kk, a].reshape(2 * TOK, 256), preferred_element_type=F32).astype(BF)
            first, second = rows[:, :128], rows[:, 128:]
            at = a * 512 + kk * 256
            out_ref[:, at : at + 128] = jnp.where(half == 0, first, second)
            out_ref[:, at + 128 : at + 256] = jnp.where(half == 0, second, first)

    for i in range(5):
        kv_copy(i).wait_send()
    q_copy.wait_send()
    for up, s in w_steps:
        for j in w_parts(up, s):
            w_copy(up, s, j).wait_send()
            if j == 0:
                w_share(up, s).wait_send()
    for s in range(2):
        for j in range(4):
            h_to_partner(s, j).wait_send()
            h_to_sibling(s, j).wait_send()
            h_forward(s, j).wait_send()
    for s in range(2):
        for a in range(2):
            for i in range(7):
                y_copy(s, a, i).wait_send()

    def sent(i, _):
        m_copy(i).wait_send()
        for s in range(2):
            for e in range(2):
                g_copy(s, e, i).wait_send()
        return 0

    lax.fori_loop(1, NC, sent, 0)


def local(queries, key_value_vectors, out_weight, doc_lengths, shard_of):
    meta = shard_of.reshape(2, 128)
    dma = pltpu.SemaphoreType.DMA
    return pl.pallas_call(
        kernel,
        out_shape=jax.ShapeDtypeStruct((TOK, 1024), BF),
        in_specs=[pl.BlockSpec(memory_space=pl.ANY)] * 4 + [pl.BlockSpec(memory_space=pltpu.SMEM)],
        out_specs=pl.BlockSpec(memory_space=pltpu.VMEM),
        scratch_shapes=[
            pltpu.VMEM((2, TOK, GW), BF),
            pltpu.VMEM((6, TOK, 256), BF),
            pltpu.VMEM((6, TOK, 256), BF),
            pltpu.VMEM((2, TOK, NK), F32),
            pltpu.VMEM((2, 2, TOK, 2 * GW), BF),
            pltpu.VMEM((NT, 2 * GW, 256), BF),
            pltpu.VMEM((2, NT, 2, 2, TOK, 128), BF),
            pltpu.VMEM((2, 2, 7, TOK, 128), BF),
            pltpu.VMEM((2, 2, NC, 32, 256), BF),
            pltpu.VMEM((2, 2, NC, 32, 256), BF),
            pltpu.VMEM((2, 512, TOK), BF),
            pltpu.VMEM((TOK, 512), BF),
            pltpu.VMEM((NC, 2, 128), jnp.int32),
            pltpu.SMEM((NC, 2, 128), jnp.int32),
            dma((5,)),
            dma((NC,)), dma((NC,)),
            dma((1,)), dma((1,)),
            dma((5,)), dma((6,)),
            dma((8, 3)), dma((8, 3)),
            dma((3, 2, 4)), dma((3, 2, 4)),
            dma((2, 2, 7)), dma((2, 2, 7)),
            dma((2, 2, NC)), dma((2, 2, NC)),
        ],
        compiler_params=pltpu.CompilerParams(
            collective_id=0, has_side_effects=True, vmem_limit_bytes=56 * 1024 * 1024
        ),
        cost_estimate=pl.CostEstimate(flops=7_000_000_000, bytes_accessed=4_000_000, transcendentals=5_000_000),
    )(queries, key_value_vectors, out_weight, meta, doc_lengths)


def solution(mesh):
    placed = (
        P(("dp", "ctx"), "tp"),
        P(("dp", "ctx"), "tp"),
        P("tp", "ctx"),
        P("dp"),
        P(("dp", "ctx")),
    )
    return jax.shard_map(
        local, mesh=mesh, in_specs=placed, out_specs=P(("dp", "ctx"), "tp"), check_vma=False
    )
```

```python
import math

import jax
import jax.numpy as jnp
from jax import lax
from jax.experimental import pallas as pl
from jax.experimental.pallas import tpu as pltpu
from jax.sharding import PartitionSpec as P

MESH = pl.DeviceIdType.MESH
BF = jnp.bfloat16
F32 = jnp.float32
HS = 128
TOK = 256
GH = 8
GW = GH * HS
NK = 5 * TOK
SCALE = math.log2(math.e) / math.sqrt(HS)
NZ = 8
NC = 16
NT = 4
UP, DOWN = 3, 5
SHARED = 608
BOTH = 2 * GW - 2 * SHARED


def mult(value, of):
    return pl.multiple_of(value, of)


def kernel(
    q_ref, kv_ref, w_ref, meta_ref, len_ref, out_ref,
    qbuf, kvb, vo, bias, hbuf, wbuf, pbuf, rbuf, xsend, xrecv, sbuf, gbuf, sel, take, mbuf, msm,
    loc, m_s, m_r, q_s, q_r, kv_s, kv_r, w_s, w_r, h_s, h_r, y_s, y_r, x_s, x_r, g_s, g_r,
):
    x = lax.axis_index("dp")
    c = lax.axis_index("ctx")
    t = lax.axis_index("tp")
    z = c // 2
    k = lax.rem(c, 2)
    xp = lax.rem(x, 2)
    xq = x + 1 - 2 * xp
    sib = c + 1 - 2 * k
    xs = 3 - x
    half = lax.rem(x + x // 2, 2)
    upper = x // 2

    def remote(src, dst, send, recv, where):
        return pltpu.make_async_remote_copy(
            src_ref=src, dst_ref=dst, send_sem=send, recv_sem=recv, device_id=where, device_id_type=MESH
        )

    barrier = pltpu.get_barrier_semaphore()

    def greet_ctx(i, _):
        pl.semaphore_signal(barrier, inc=1, device_id={"ctx": lax.rem(c + i, NC)}, device_id_type=MESH)
        return 0

    lax.fori_loop(1, NC, greet_ctx, 0)
    for i in range(1, NT):
        pl.semaphore_signal(barrier, inc=1, device_id={"tp": lax.rem(t + i, NT)}, device_id_type=MESH)
    pl.semaphore_signal(barrier, inc=1, device_id={"dp": xq}, device_id_type=MESH)
    pl.semaphore_signal(barrier, inc=1, device_id={"dp": xs}, device_id_type=MESH)
    pl.semaphore_wait(barrier, NC - 1 + NT - 1 + 2)

    def kv_copy(i):
        if i == 0:
            g, slot, to = 1 - k, 4 + k, sib
        else:
            hop, g = (i + 1) // 2, (i + 1) % 2
            slot, to = 4 - 2 * hop + k, 2 * lax.rem(z + hop, NZ) + g
        return remote(
            kv_ref.at[:, pl.ds(mult(g * 256, 256), 256)], kvb.at[slot], kv_s.at[i], kv_r.at[slot], {"ctx": to}
        )

    def kv_arrival(slot):
        return remote(kvb.at[slot], kvb.at[slot], kv_s.at[0], kv_r.at[slot], {"ctx": sib})

    q_copy = remote(
        q_ref.at[:, pl.ds(mult((1 - k) * GW, GW), GW)], qbuf.at[k], q_s.at[0], q_r.at[0], {"ctx": sib}
    )
    q_arrival = remote(qbuf.at[1 - k], qbuf.at[1 - k], q_s.at[0], q_r.at[0], {"ctx": sib})

    def w_rows(j, mine=True):
        if j == 0:
            return pl.ds(mult((upper if mine else 1 - upper) * SHARED, 16), SHARED)
        return pl.ds(2 * SHARED, BOTH)

    def w_place(zz, rows):
        return wbuf.at[zz // 2, rows, pl.ds(mult(lax.rem(zz, 2) * 128, 128), 128)]

    def w_block(up, s):
        return lax.rem(z + (NZ - s if up else s), NZ)

    def w_index(up, s):
        return (0 if up else UP) + s - 1

    def w_copy(up, s, j):
        zz = w_block(up, s - 1)
        to = 2 * lax.rem(z + (1 if up else NZ - 1), NZ) + k
        n = w_index(up, s)
        place = w_place(zz, w_rows(j))
        src = w_ref.at[w_rows(j), pl.ds(mult(half * 128, 128), 128)] if s == 1 else place
        return remote(src, place, w_s.at[n, j], w_r.at[n, j], {"ctx": to})

    def w_share(up, s):
        n = w_index(up, s)
        place = w_place(w_block(up, s), w_rows(0))
        return remote(place, place, w_s.at[n, 2], w_r.at[n, 2], {"dp": xs})

    def w_shared(up, s):
        n = w_index(up, s)
        place = w_place(w_block(up, s), w_rows(0, False))
        return remote(place, place, w_s.at[n, 2], w_r.at[n, 2], {"dp": xs})

    def w_parts(up, s):
        return (1,) if up and s == UP else (0,) if not up and s == DOWN else (0, 1)

    def w_start(up, s, j):
        if s <= (UP if up else DOWN) and j in w_parts(up, s):
            w_copy(up, s, j).start()

    def w_arrived(up, s, j):
        n = w_index(up, s)
        place = w_place(w_block(up, s), w_rows(j))
        remote(place, place, w_s.at[n, j], w_r.at[n, j], {"ctx": sib}).wait_recv()
        w_start(up, s + 1, j)
        if j == 0:
            w_share(up, s).start()

    w_steps = [(True, s) for s in range(1, UP + 1)] + [(False, s) for s in range(1, DOWN + 1)]

    local_copies = [
        pltpu.make_async_copy(q_ref.at[:, pl.ds(mult(k * GW, GW), GW)], qbuf.at[k], loc.at[0]),
        pltpu.make_async_copy(kv_ref.at[:, pl.ds(mult(k * 256, 256), 256)], kvb.at[4 + k], loc.at[1]),
        pltpu.make_async_copy(w_ref.at[:, pl.ds(mult(half * 128, 128), 128)],
                              wbuf.at[z // 2, :, pl.ds(mult(lax.rem(z, 2) * 128, 128), 128)], loc.at[2]),
        pltpu.make_async_copy(meta_ref, mbuf.at[c], loc.at[3]),
    ]

    def m_copy(i):
        return remote(meta_ref, mbuf.at[c], m_s.at[i], m_r.at[i], {"ctx": lax.rem(c + i, NC)})

    kv_copy(0).start()
    w_copy(False, 1, 0).start()
    kv_copy(1).start()
    kv_copy(2).start()

    @pl.when(k == 1)
    def _():
        kv_copy(3).start()
        kv_copy(4).start()
        w_copy(True, 1, 0).start()

    @pl.when(k == 0)
    def _():
        w_copy(True, 1, 0).start()
        kv_copy(3).start()
        kv_copy(4).start()

    w_copy(False, 1, 1).start()
    w_copy(True, 1, 1).start()
    q_copy.start()
    for copy in local_copies:
        copy.start()

    def m_send(i, _):
        m_copy(i).start()
        return 0

    lax.fori_loop(1, NC, m_send, 0)

    ends = []
    total = jnp.int32(0)
    for d in range(8):
        total = total + len_ref[d]
        ends.append(total)
    for s in range(2):
        base = z * 512 + s * 256
        rows = lax.broadcasted_iota(jnp.int32, (TOK, 1), 0)
        start = jnp.zeros((TOK, 1), jnp.int32)
        for e in ends:
            start = jnp.where(rows + base >= e, e, start)
        keys = lax.broadcasted_iota(jnp.int32, (TOK, NK), 1)
        seen = (keys <= rows + 1024) & (keys >= start - (base - 1024))
        bias[s] = jnp.where(seen, 0.0, -1e30).astype(F32)

    kv_arrival(2).wait_recv()
    kv_arrival(3).wait_recv()

    for copy in local_copies:
        copy.wait()
    q_arrival.wait_recv()
    kv_arrival(5 - k).wait_recv()
    def widen(slot, count):
        vo[slot : slot + count, :, 0:HS] = kvb[slot : slot + count, :, HS:]
        vo[slot : slot + count, :, HS:] = jnp.ones((count, TOK, HS), BF)

    widen(2, 4)
    w_arrived(False, 1, 0)
    w_arrived(False, 1, 1)
    w_arrived(False, 2, 0)
    kv_arrival(1).wait_recv()
    widen(1, 1)

    def h_lanes(j, kk):
        return pl.ds(mult(kk * GW + j * 256, 256), 256)

    def h_to_partner(s, j):
        return remote(hbuf.at[0, s, :, h_lanes(j, k)], hbuf.at[1, s, :, h_lanes(j, k)],
                      h_s.at[0, s, j], h_r.at[0, s, j], {"dp": xq})

    def h_to_sibling(s, j):
        place = hbuf.at[0, s, :, h_lanes(j, k)]
        return remote(place, place, h_s.at[1, s, j], h_r.at[1, s, j], {"ctx": sib})

    def h_forward(s, j):
        place = hbuf.at[1, s, :, h_lanes(j, k)]
        return remote(place, place, h_s.at[2, s, j], h_r.at[2, s, j], {"ctx": sib})

    def h_arrival(s, j, way):
        place = hbuf.at[1, s, :, h_lanes(j, k)] if way == 0 else hbuf.at[way - 1, s, :, h_lanes(j, 1 - k)]
        return remote(place, place, h_s.at[way, s, j], h_r.at[way, s, j], {"ctx": sib})

    def attend(s, j):
        keys = kvb[s : s + 5, :, 0:HS].reshape(NK, HS)
        values = vo[s : s + 5].reshape(NK, 2 * HS)
        heads = (2 * j, 2 * j + 1)
        scores = [
            lax.dot_general(qbuf[s, :, h * HS : (h + 1) * HS], keys, (((1,), (1,)), ((), ())),
                            preferred_element_type=F32)
            for h in heads
        ]
        for h, score in zip(heads, scores):
            score = score * SCALE + bias[s]
            weights = jnp.exp2(score - jnp.max(score, axis=1, keepdims=True)).astype(BF)
            mixed = jnp.dot(weights, values, preferred_element_type=F32)
            hbuf[0, s, :, pl.ds(mult(k * GW + h * HS, HS), HS)] = (mixed[:, :HS] / mixed[:, HS:]).astype(BF)
        h_to_partner(s, j).start()
        h_to_sibling(s, j).start()

    def h_pass_on(s, j):
        h_arrival(s, j, 0).wait_recv()
        h_forward(s, j).start()

    attend(1, 0)
    w_arrived(False, 2, 1)
    attend(1, 1)
    w_arrived(True, 1, 0)
    attend(1, 2)
    attend(1, 3)
    w_arrived(False, 3, 0)
    kv_arrival(0).wait_recv()
    widen(0, 1)
    attend(0, 0)
    h_pass_on(1, 0)
    w_arrived(True, 1, 1)
    w_arrived(False, 3, 1)
    attend(0, 1)
    h_pass_on(1, 1)
    attend(0, 2)
    h_pass_on(1, 2)
    w_arrived(True, 2, 0)
    w_arrived(False, 4, 0)
    attend(0, 3)
    h_pass_on(1, 3)

    def m_wait(i, _):
        src = lax.rem(c + NC - i, NC)
        remote(mbuf.at[src], mbuf.at[src], m_s.at[i], m_r.at[i], {"ctx": sib}).wait_recv()
        return 0

    lax.fori_loop(1, NC, m_wait, 0)
    table = pltpu.make_async_copy(mbuf, msm, loc.at[4])
    table.start()
    table.wait()

    def owner(n, b):
        return msm[n, b // 8, (b % 8) * 16]

    lane = lax.broadcasted_iota(jnp.int32, (1, TOK), 1)
    for s in range(2):
        owners = [owner(2 * z + s, b) for b in range(16)]
        wanted = jnp.zeros((1, TOK), jnp.int32)
        for b in range(16):
            second = jnp.int32(0)
            for e in range(b):
                second = second + jnp.where(owners[e] == owners[b], 16, 0)
            slot = owners[b] - c
            slot = jnp.where(slot < 0, slot + NC, slot)
            wanted = jnp.where(lane // 16 == b, slot * 32 + second, wanted)
        wanted = wanted + lax.rem(lane, 16)
        row = lax.broadcasted_iota(jnp.int32, (512, TOK), 0)
        sel[s] = jnp.where(row == wanted, 1.0, 0.0).astype(BF)

    counts = []
    count = jnp.int32(0)
    for n in range(NC):
        any_block = jnp.int32(0)
        for b in range(16):
            any_block = jnp.maximum(any_block, jnp.where(owner(n, b) == c, 1, 0))
        count = count + any_block
        counts.append(count)

    def place(r, _):
        src = jnp.int32(0)
        for n in range(NC - 1):
            src = src + jnp.where(counts[n] <= r, 1, 0)
        row = lax.broadcasted_iota(jnp.int32, (32, 512), 0)
        column = lax.broadcasted_iota(jnp.int32, (32, 512), 1)
        take[pl.ds(mult(r * 32, 32), 32), :] = jnp.where(column == row + src * 32, 1.0, 0.0).astype(BF)
        return 0

    lax.fori_loop(0, 8, place, 0)

    def column_half(o):
        return lax.rem(z + o, 2)

    def piece(e, s):
        return pl.ds(s * TOK, TOK) if e == 1 else pl.ds(0, 2 * TOK)

    pieces = ((0, 0), (1, 0), (1, 1))

    def y_copy(o, e, s, i):
        tt = lax.rem(t + 1 + i, NT)
        return remote(pbuf.at[o, e, tt, piece(e, s)], rbuf.at[o, e, i, piece(e, s)],
                      y_s.at[o, e, s, i], y_r.at[o, e, s, i], {"tp": tt})

    def product(o, e):
        def one(i, _):
            tt = lax.rem(t + 1 + i, NT)
            columns = wbuf[tt, :, pl.ds(mult(column_half(o) * 128, 128), 128)]
            part = jnp.dot(hbuf[e].reshape(2 * TOK, 2 * GW), columns, preferred_element_type=F32)
            pbuf[o, e, tt] = part.astype(BF)

            @pl.when(i < NT - 1)
            def _():
                y_copy(o, e, 0, i).start()

            return 0

        lax.fori_loop(0, NT, one, 0)
        if e == 1:
            for i in range(NT - 1):
                y_copy(o, e, 1, i).start()

    def summed(o, e, s):
        total = pbuf[o, e, t, piece(e, s)].astype(F32)
        for i in range(NT - 1):
            place = rbuf.at[o, e, i, piece(e, s)]
            remote(place, place, y_s.at[o, e, s, i], y_r.at[o, e, s, i], {"ctx": sib}).wait_recv()
            total = total + rbuf[o, e, i, piece(e, s)].astype(F32)
        return total.astype(BF)

    def x_return(o, s):
        return remote(xsend.at[o, s], xrecv.at[o, s], x_s.at[o, s], x_r.at[o, s], {"dp": xq})

    def shards(e, s):
        return pl.ds(s, 1) if e == 1 else pl.ds(0, 2)

    def g_copy(o, e, s, i):
        a = column_half(o)
        return remote(sbuf.at[o, e, i, shards(e, s)], gbuf.at[k, a, e, z, shards(e, s)],
                      g_s.at[a, e, s, i], g_r.at[a, e, s, i], {"ctx": lax.rem(c + i, NC)})

    def pick(o, e, s, rows):
        picked = jnp.dot(sel[s], rows, preferred_element_type=F32)
        sbuf[o, e, :, s] = picked.astype(BF).reshape(NC, 32, 128)

    def send_packed(o, e, s):
        def send(i, _):
            g_copy(o, e, s, i).start()
            return 0

        lax.fori_loop(1, NC, send, 0)
        gbuf[k, column_half(o), e, z, shards(e, s)] = sbuf[o, e, 0, shards(e, s)]

    def pack(o):
        rows = summed(o, 0, 0)
        for s in range(2):
            pick(o, 0, s, rows[s * TOK : (s + 1) * TOK])
        send_packed(o, 0, 0)

    def give_back(o, s):
        xsend[o, s] = summed(o, 1, s)
        x_return(o, s).start()

    def pack_returned(o, s):
        x_return(o, s).wait_recv()
        pick(o, 1, s, xrecv[o, s])
        send_packed(o, 1, s)

    w_arrived(False, 4, 1)
    w_arrived(True, 2, 1)
    for up, s in w_steps:
        if s % 2 == 0:
            w_shared(up, s).wait_recv()
    for s in range(2):
        for j in range(4):
            h_arrival(s, j, 1).wait_recv()
    h_pass_on(0, 0)
    product(0, 0)
    h_pass_on(0, 1)
    w_arrived(False, 5, 0)
    w_arrived(True, 3, 1)
    h_pass_on(0, 2)
    h_pass_on(0, 3)
    for s in range(2):
        for j in range(4):
            h_arrival(s, j, 2).wait_recv()
    product(0, 1)
    for up, s in w_steps:
        if s % 2 == 1 and 0 in w_parts(up, s):
            w_shared(up, s).wait_recv()
    pack(0)
    give_back(0, 0)
    product(1, 0)
    give_back(0, 1)
    pack_returned(0, 0)
    product(1, 1)
    pack_returned(0, 1)
    pack(1)
    give_back(1, 0)
    give_back(1, 1)
    pack_returned(1, 0)
    pack_returned(1, 1)

    for e in range(2):
        for a in range(2):
            def g_wait(i, _):
                src = lax.rem(c + NC - i, NC)
                for s in range(2 if e == 1 else 1):
                    place = gbuf.at[lax.rem(src, 2), a, e, src // 2, shards(e, s)]
                    remote(place, place, g_s.at[a, e, s, i], g_r.at[a, e, s, i], {"ctx": sib}).wait_recv()
                return 0

            lax.fori_loop(1, NC, g_wait, 0)
            for kk in range(2):
                rows = jnp.dot(take[...], gbuf[kk, a, e].reshape(2 * TOK, 128), preferred_element_type=F32)
                at = a * 512 + kk * 256 + (half if e == 0 else 1 - half) * 128
                out_ref[:, pl.ds(mult(at, 128), 128)] = rows.astype(BF)

    for i in range(5):
        kv_copy(i).wait_send()
    q_copy.wait_send()
    for up, s in w_steps:
        for j in w_parts(up, s):
            w_copy(up, s, j).wait_send()
            if j == 0:
                w_share(up, s).wait_send()
    for s in range(2):
        for j in range(4):
            h_to_partner(s, j).wait_send()
            h_to_sibling(s, j).wait_send()
            h_forward(s, j).wait_send()
    for o in range(2):
        for s in range(2):
            x_return(o, s).wait_send()
        for e, s in pieces:
            for i in range(NT - 1):
                y_copy(o, e, s, i).wait_send()

    def sent(i, _):
        m_copy(i).wait_send()
        for o in range(2):
            for e, s in pieces:
                g_copy(o, e, s, i).wait_send()
        return 0

    lax.fori_loop(1, NC, sent, 0)


def local(queries, key_value_vectors, out_weight, doc_lengths, shard_of):
    meta = shard_of.reshape(2, 128)
    dma = pltpu.SemaphoreType.DMA
    return pl.pallas_call(
        kernel,
        out_shape=jax.ShapeDtypeStruct((TOK, 1024), BF),
        in_specs=[pl.BlockSpec(memory_space=pl.ANY)] * 4 + [pl.BlockSpec(memory_space=pltpu.SMEM)],
        out_specs=pl.BlockSpec(memory_space=pltpu.VMEM),
        scratch_shapes=[
            pltpu.VMEM((2, TOK, GW), BF),
            pltpu.VMEM((6, TOK, 256), BF),
            pltpu.VMEM((6, TOK, 256), BF),
            pltpu.VMEM((2, TOK, NK), F32),
            pltpu.VMEM((2, 2, TOK, 2 * GW), BF),
            pltpu.VMEM((NT, 2 * GW, 256), BF),
            pltpu.VMEM((2, 2, NT, 2 * TOK, 128), BF),
            pltpu.VMEM((2, 2, NT - 1, 2 * TOK, 128), BF),
            pltpu.VMEM((2, 2, TOK, 128), BF),
            pltpu.VMEM((2, 2, TOK, 128), BF),
            pltpu.VMEM((2, 2, NC, 2, 32, 128), BF),
            pltpu.VMEM((2, 2, 2, NZ, 2, 32, 128), BF),
            pltpu.VMEM((2, 512, TOK), BF),
            pltpu.VMEM((TOK, 512), BF),
            pltpu.VMEM((NC, 2, 128), jnp.int32),
            pltpu.SMEM((NC, 2, 128), jnp.int32),
            dma((5,)),
            dma((NC,)), dma((NC,)),
            dma((1,)), dma((1,)),
            dma((5,)), dma((6,)),
            dma((8, 3)), dma((8, 3)),
            dma((3, 2, 4)), dma((3, 2, 4)),
            dma((2, 2, 2, 3)), dma((2, 2, 2, 3)),
            dma((2, 2)), dma((2, 2)),
            dma((2, 2, 2, NC)), dma((2, 2, 2, NC)),
        ],
        compiler_params=pltpu.CompilerParams(
            collective_id=0, has_side_effects=True, vmem_limit_bytes=56 * 1024 * 1024
        ),
        cost_estimate=pl.CostEstimate(flops=7_000_000_000, bytes_accessed=4_000_000, transcendentals=5_000_000),
    )(queries, key_value_vectors, out_weight, meta, doc_lengths)


def solution(mesh):
    placed = (
        P(("dp", "ctx"), "tp"),
        P(("dp", "ctx"), "tp"),
        P("tp", "ctx"),
        P("dp"),
        P(("dp", "ctx")),
    )
    return jax.shard_map(
        local, mesh=mesh, in_specs=placed, out_specs=P(("dp", "ctx"), "tp"), check_vma=False
    )
```

```python
import math

import jax
import jax.numpy as jnp
from jax import lax
from jax.experimental import pallas as pl
from jax.experimental.pallas import tpu as pltpu
from jax.sharding import PartitionSpec as P

MESH = pl.DeviceIdType.MESH
BF = jnp.bfloat16
F32 = jnp.float32
HS = 128
TOK = 256
GH = 8
GW = GH * HS
NK = 5 * TOK
SCALE = math.log2(math.e) / math.sqrt(HS)
NZ = 8
NC = 16
NT = 4
UP, DOWN = 3, 5
SHARED = 608
BOTH = 2 * GW - 2 * SHARED


def mult(value, of):
    return pl.multiple_of(value, of)


def kernel(
    q_ref, kv_ref, w_ref, meta_ref, len_ref, out_ref,
    qbuf, kvb, vo, bias, hbuf, wbuf, pbuf, rbuf, xsend, xrecv, sbuf, gbuf, sel, take, mbuf, msm,
    loc, m_s, m_r, q_s, q_r, kv_s, kv_r, w_s, w_r, h_s, h_r, y_s, y_r, x_s, x_r, g_s, g_r,
):
    x = lax.axis_index("dp")
    c = lax.axis_index("ctx")
    t = lax.axis_index("tp")
    z = c // 2
    k = lax.rem(c, 2)
    xp = lax.rem(x, 2)
    xq = x + 1 - 2 * xp
    sib = c + 1 - 2 * k
    xs = 3 - x
    half = lax.rem(x + x // 2, 2)
    upper = x // 2

    def remote(src, dst, send, recv, where):
        return pltpu.make_async_remote_copy(
            src_ref=src, dst_ref=dst, send_sem=send, recv_sem=recv, device_id=where, device_id_type=MESH
        )

    barrier = pltpu.get_barrier_semaphore()

    def greet_ctx(i, _):
        pl.semaphore_signal(barrier, inc=1, device_id={"ctx": lax.rem(c + i, NC)}, device_id_type=MESH)
        return 0

    lax.fori_loop(1, NC, greet_ctx, 0)
    for i in range(1, NT):
        pl.semaphore_signal(barrier, inc=1, device_id={"tp": lax.rem(t + i, NT)}, device_id_type=MESH)
    pl.semaphore_signal(barrier, inc=1, device_id={"dp": xq}, device_id_type=MESH)
    pl.semaphore_signal(barrier, inc=1, device_id={"dp": xs}, device_id_type=MESH)
    pl.semaphore_wait(barrier, NC - 1 + NT - 1 + 2)

    def kv_copy(i):
        if i == 0:
            g, slot, to = 1 - k, 4 + k, sib
        else:
            hop, g = (i + 1) // 2, (i + 1) % 2
            slot, to = 4 - 2 * hop + k, 2 * lax.rem(z + hop, NZ) + g
        return remote(
            kv_ref.at[:, pl.ds(mult(g * 256, 256), 256)], kvb.at[slot], kv_s.at[i], kv_r.at[slot], {"ctx": to}
        )

    def kv_arrival(slot):
        return remote(kvb.at[slot], kvb.at[slot], kv_s.at[0], kv_r.at[slot], {"ctx": sib})

    q_copy = remote(
        q_ref.at[:, pl.ds(mult((1 - k) * GW, GW), GW)], qbuf.at[k], q_s.at[0], q_r.at[0], {"ctx": sib}
    )
    q_arrival = remote(qbuf.at[1 - k], qbuf.at[1 - k], q_s.at[0], q_r.at[0], {"ctx": sib})

    def w_rows(j, mine=True):
        if j == 0:
            return pl.ds(mult((upper if mine else 1 - upper) * SHARED, 16), SHARED)
        return pl.ds(2 * SHARED, BOTH)

    def w_place(zz, rows):
        return wbuf.at[zz // 2, rows, pl.ds(mult(lax.rem(zz, 2) * 128, 128), 128)]

    def w_block(up, s):
        return lax.rem(z + (NZ - s if up else s), NZ)

    def w_index(up, s):
        return (0 if up else UP) + s - 1

    def w_copy(up, s, j):
        zz = w_block(up, s - 1)
        to = 2 * lax.rem(z + (1 if up else NZ - 1), NZ) + k
        n = w_index(up, s)
        place = w_place(zz, w_rows(j))
        src = w_ref.at[w_rows(j), pl.ds(mult(half * 128, 128), 128)] if s == 1 else place
        return remote(src, place, w_s.at[n, j], w_r.at[n, j], {"ctx": to})

    def w_share(up, s):
        n = w_index(up, s)
        place = w_place(w_block(up, s), w_rows(0))
        return remote(place, place, w_s.at[n, 2], w_r.at[n, 2], {"dp": xs})

    def w_shared(up, s):
        n = w_index(up, s)
        place = w_place(w_block(up, s), w_rows(0, False))
        return remote(place, place, w_s.at[n, 2], w_r.at[n, 2], {"dp": xs})

    def w_parts(up, s):
        return (1,) if up and s == UP else (0,) if not up and s == DOWN else (0, 1)

    def w_start(up, s, j):
        if s <= (UP if up else DOWN) and j in w_parts(up, s):
            w_copy(up, s, j).start()

    def w_arrived(up, s, j):
        n = w_index(up, s)
        place = w_place(w_block(up, s), w_rows(j))
        remote(place, place, w_s.at[n, j], w_r.at[n, j], {"ctx": sib}).wait_recv()
        w_start(up, s + 1, j)
        if j == 0:
            w_share(up, s).start()

    w_steps = [(True, s) for s in range(1, UP + 1)] + [(False, s) for s in range(1, DOWN + 1)]

    local_copies = [
        pltpu.make_async_copy(q_ref.at[:, pl.ds(mult(k * GW, GW), GW)], qbuf.at[k], loc.at[0]),
        pltpu.make_async_copy(kv_ref.at[:, pl.ds(mult(k * 256, 256), 256)], kvb.at[4 + k], loc.at[1]),
        pltpu.make_async_copy(w_ref.at[:, pl.ds(mult(half * 128, 128), 128)],
                              wbuf.at[z // 2, :, pl.ds(mult(lax.rem(z, 2) * 128, 128), 128)], loc.at[2]),
        pltpu.make_async_copy(meta_ref, mbuf.at[c], loc.at[3]),
    ]

    def m_copy(i):
        return remote(meta_ref, mbuf.at[c], m_s.at[i], m_r.at[i], {"ctx": lax.rem(c + i, NC)})

    kv_copy(0).start()
    w_copy(False, 1, 0).start()
    kv_copy(1).start()
    kv_copy(2).start()

    @pl.when(k == 1)
    def _():
        kv_copy(3).start()
        kv_copy(4).start()
        w_copy(True, 1, 0).start()

    @pl.when(k == 0)
    def _():
        w_copy(True, 1, 0).start()
        kv_copy(3).start()
        kv_copy(4).start()

    w_copy(False, 1, 1).start()
    w_copy(True, 1, 1).start()
    q_copy.start()
    for copy in local_copies:
        copy.start()

    def m_send(i, _):
        m_copy(i).start()
        return 0

    lax.fori_loop(1, NC, m_send, 0)

    ends = []
    total = jnp.int32(0)
    for d in range(8):
        total = total + len_ref[d]
        ends.append(total)
    for s in range(2):
        base = z * 512 + s * 256
        rows = lax.broadcasted_iota(jnp.int32, (TOK, 1), 0)
        start = jnp.zeros((TOK, 1), jnp.int32)
        for e in ends:
            start = jnp.where(rows + base >= e, e, start)
        keys = lax.broadcasted_iota(jnp.int32, (TOK, NK), 1)
        seen = (keys <= rows + 1024) & (keys >= start - (base - 1024))
        bias[s] = jnp.where(seen, 0.0, -1e30).astype(F32)

    kv_arrival(2).wait_recv()
    kv_arrival(3).wait_recv()

    for copy in local_copies:
        copy.wait()
    q_arrival.wait_recv()
    kv_arrival(5 - k).wait_recv()
    def widen(slot, count):
        vo[slot : slot + count, :, 0:HS] = kvb[slot : slot + count, :, HS:]
        vo[slot : slot + count, :, HS:] = jnp.ones((count, TOK, HS), BF)

    widen(2, 4)
    w_arrived(False, 1, 0)
    w_arrived(False, 1, 1)
    kv_arrival(1).wait_recv()
    widen(1, 1)

    def h_lanes(j, kk):
        return pl.ds(mult(kk * GW + j * 256, 256), 256)

    def h_to_partner(s, j):
        return remote(hbuf.at[0, s, :, h_lanes(j, k)], hbuf.at[1, s, :, h_lanes(j, k)],
                      h_s.at[0, s, j], h_r.at[0, s, j], {"dp": xq})

    def h_to_sibling(s, j):
        place = hbuf.at[0, s, :, h_lanes(j, k)]
        return remote(place, place, h_s.at[1, s, j], h_r.at[1, s, j], {"ctx": sib})

    def h_forward(s, j):
        place = hbuf.at[1, s, :, h_lanes(j, k)]
        return remote(place, place, h_s.at[2, s, j], h_r.at[2, s, j], {"ctx": sib})

    def h_arrival(s, j, way):
        place = hbuf.at[1, s, :, h_lanes(j, k)] if way == 0 else hbuf.at[way - 1, s, :, h_lanes(j, 1 - k)]
        return remote(place, place, h_s.at[way, s, j], h_r.at[way, s, j], {"ctx": sib})

    def attend(s, j):
        keys = kvb[s : s + 5, :, 0:HS].reshape(NK, HS)
        values = vo[s : s + 5].reshape(NK, 2 * HS)
        heads = (2 * j, 2 * j + 1)
        scores = [
            lax.dot_general(qbuf[s, :, h * HS : (h + 1) * HS], keys, (((1,), (1,)), ((), ())),
                            preferred_element_type=F32)
            for h in heads
        ]
        for h, score in zip(heads, scores):
            score = score * SCALE + bias[s]
            weights = jnp.exp2(score - jnp.max(score, axis=1, keepdims=True)).astype(BF)
            mixed = jnp.dot(weights, values, preferred_element_type=F32)
            hbuf[0, s, :, pl.ds(mult(k * GW + h * HS, HS), HS)] = (mixed[:, :HS] / mixed[:, HS:]).astype(BF)
        h_to_partner(s, j).start()
        h_to_sibling(s, j).start()

    def h_pass_on(s, j):
        h_arrival(s, j, 0).wait_recv()
        h_forward(s, j).start()

    attend(1, 0)
    w_arrived(False, 2, 0)
    w_arrived(False, 2, 1)
    attend(1, 1)
    w_arrived(True, 1, 0)
    attend(1, 2)
    attend(1, 3)
    w_arrived(False, 3, 0)
    kv_arrival(0).wait_recv()
    widen(0, 1)
    attend(0, 0)
    h_pass_on(1, 0)
    w_arrived(True, 1, 1)
    w_arrived(False, 3, 1)
    attend(0, 1)
    h_pass_on(1, 1)
    attend(0, 2)
    h_pass_on(1, 2)
    w_arrived(True, 2, 0)
    w_arrived(False, 4, 0)
    attend(0, 3)
    h_pass_on(1, 3)

    def m_wait(i, _):
        src = lax.rem(c + NC - i, NC)
        remote(mbuf.at[src], mbuf.at[src], m_s.at[i], m_r.at[i], {"ctx": sib}).wait_recv()
        return 0

    lax.fori_loop(1, NC, m_wait, 0)
    table = pltpu.make_async_copy(mbuf, msm, loc.at[4])
    table.start()
    table.wait()

    def owner(n, b):
        return msm[n, b // 8, (b % 8) * 16]

    lane = lax.broadcasted_iota(jnp.int32, (1, TOK), 1)
    for s in range(2):
        owners = [owner(2 * z + s, b) for b in range(16)]
        wanted = jnp.zeros((1, TOK), jnp.int32)
        for b in range(16):
            second = jnp.int32(0)
            for e in range(b):
                second = second + jnp.where(owners[e] == owners[b], 16, 0)
            slot = owners[b] - c
            slot = jnp.where(slot < 0, slot + NC, slot)
            wanted = jnp.where(lane // 16 == b, slot * 32 + second, wanted)
        wanted = wanted + lax.rem(lane, 16)
        row = lax.broadcasted_iota(jnp.int32, (512, TOK), 0)
        sel[s] = jnp.where(row == wanted, 1.0, 0.0).astype(BF)

    counts = []
    count = jnp.int32(0)
    for n in range(NC):
        any_block = jnp.int32(0)
        for b in range(16):
            any_block = jnp.maximum(any_block, jnp.where(owner(n, b) == c, 1, 0))
        count = count + any_block
        counts.append(count)

    def place(r, _):
        src = jnp.int32(0)
        for n in range(NC - 1):
            src = src + jnp.where(counts[n] <= r, 1, 0)
        row = lax.broadcasted_iota(jnp.int32, (32, 512), 0)
        column = lax.broadcasted_iota(jnp.int32, (32, 512), 1)
        take[pl.ds(mult(r * 32, 32), 32), :] = jnp.where(column == row + src * 32, 1.0, 0.0).astype(BF)
        return 0

    lax.fori_loop(0, 8, place, 0)

    def column_half(o):
        return lax.rem(z + o, 2)

    def piece(e, s):
        return pl.ds(s * TOK, TOK) if e == 1 else pl.ds(0, 2 * TOK)

    pieces = ((0, 0), (1, 0), (1, 1))

    def y_copy(o, e, s, i):
        tt = lax.rem(t + 1 + i, NT)
        return remote(pbuf.at[o, e, tt, piece(e, s)], rbuf.at[o, e, i, piece(e, s)],
                      y_s.at[o, e, s, i], y_r.at[o, e, s, i], {"tp": tt})

    def product(o, e):
        def one(i, _):
            tt = lax.rem(t + 1 + i, NT)
            columns = wbuf[tt, :, pl.ds(mult(column_half(o) * 128, 128), 128)]
            part = jnp.dot(hbuf[e].reshape(2 * TOK, 2 * GW), columns, preferred_element_type=F32)
            pbuf[o, e, tt] = part.astype(BF)

            @pl.when(i < NT - 1)
            def _():
                y_copy(o, e, 0, i).start()

            return 0

        lax.fori_loop(0, NT, one, 0)
        if e == 1:
            for i in range(NT - 1):
                y_copy(o, e, 1, i).start()

    def summed(o, e, s):
        total = pbuf[o, e, t, piece(e, s)].astype(F32)
        for i in range(NT - 1):
            place = rbuf.at[o, e, i, piece(e, s)]
            remote(place, place, y_s.at[o, e, s, i], y_r.at[o, e, s, i], {"ctx": sib}).wait_recv()
            total = total + rbuf[o, e, i, piece(e, s)].astype(F32)
        return total.astype(BF)

    def x_return(o, s):
        return remote(xsend.at[o, s], xrecv.at[o, s], x_s.at[o, s], x_r.at[o, s], {"dp": xq})

    def shards(e, s):
        return pl.ds(s, 1) if e == 1 else pl.ds(0, 2)

    def g_copy(o, e, s, i):
        a = column_half(o)
        return remote(sbuf.at[o, e, i, shards(e, s)], gbuf.at[k, a, e, z, shards(e, s)],
                      g_s.at[a, e, s, i], g_r.at[a, e, s, i], {"ctx": lax.rem(c + i, NC)})

    def pick(o, e, s, rows):
        picked = jnp.dot(sel[s], rows, preferred_element_type=F32)
        sbuf[o, e, :, s] = picked.astype(BF).reshape(NC, 32, 128)

    def send_packed(o, e, s):
        def send(i, _):
            g_copy(o, e, s, i).start()
            return 0

        lax.fori_loop(1, NC, send, 0)
        gbuf[k, column_half(o), e, z, shards(e, s)] = sbuf[o, e, 0, shards(e, s)]

    def pack(o):
        rows = summed(o, 0, 0)
        for s in range(2):
            pick(o, 0, s, rows[s * TOK : (s + 1) * TOK])
        send_packed(o, 0, 0)

    def give_back(o, s):
        xsend[o, s] = summed(o, 1, s)
        x_return(o, s).start()

    def pack_returned(o, s):
        x_return(o, s).wait_recv()
        pick(o, 1, s, xrecv[o, s])
        send_packed(o, 1, s)

    w_arrived(False, 4, 1)
    w_arrived(True, 2, 1)
    for up, s in w_steps:
        if s % 2 == 0:
            w_shared(up, s).wait_recv()
    for s in range(2):
        for j in range(4):
            h_arrival(s, j, 1).wait_recv()
    h_pass_on(0, 0)
    product(0, 0)
    h_pass_on(0, 1)
    w_arrived(False, 5, 0)
    w_arrived(True, 3, 1)
    h_pass_on(0, 2)
    h_pass_on(0, 3)
    for s in range(2):
        for j in range(4):
            h_arrival(s, j, 2).wait_recv()
    product(0, 1)
    for up, s in w_steps:
        if s % 2 == 1 and 0 in w_parts(up, s):
            w_shared(up, s).wait_recv()
    pack(0)
    product(1, 0)
    give_back(0, 0)
    give_back(0, 1)
    pack_returned(0, 0)
    product(1, 1)
    pack_returned(0, 1)
    pack(1)
    give_back(1, 0)
    give_back(1, 1)
    pack_returned(1, 0)
    pack_returned(1, 1)

    for i in range(5):
        kv_copy(i).wait_send()
    q_copy.wait_send()
    for up, s in w_steps:
        for j in w_parts(up, s):
            w_copy(up, s, j).wait_send()
            if j == 0:
                w_share(up, s).wait_send()
    for s in range(2):
        for j in range(4):
            h_to_partner(s, j).wait_send()
            h_to_sibling(s, j).wait_send()
            h_forward(s, j).wait_send()
    for o in range(2):
        for s in range(2):
            x_return(o, s).wait_send()
        for e, s in pieces:
            for i in range(NT - 1):
                y_copy(o, e, s, i).wait_send()

    def sent(i, _):
        m_copy(i).wait_send()
        for e, s in pieces:
            g_copy(0, e, s, i).wait_send()
        return 0

    lax.fori_loop(1, NC, sent, 0)

    for e in range(2):
        for a in range(2):
            def g_wait(i, _):
                src = lax.rem(c + NC - i, NC)
                for s in range(2 if e == 1 else 1):
                    place = gbuf.at[lax.rem(src, 2), a, e, src // 2, shards(e, s)]
                    remote(place, place, g_s.at[a, e, s, i], g_r.at[a, e, s, i], {"ctx": sib}).wait_recv()
                return 0

            lax.fori_loop(1, NC, g_wait, 0)
            for kk in range(2):
                rows = jnp.dot(take[...], gbuf[kk, a, e].reshape(2 * TOK, 128), preferred_element_type=F32)
                at = a * 512 + kk * 256 + (half if e == 0 else 1 - half) * 128
                out_ref[:, pl.ds(mult(at, 128), 128)] = rows.astype(BF)

    def sent_last(i, _):
        for e, s in pieces:
            g_copy(1, e, s, i).wait_send()
        return 0

    lax.fori_loop(1, NC, sent_last, 0)


def local(queries, key_value_vectors, out_weight, doc_lengths, shard_of):
    meta = shard_of.reshape(2, 128)
    dma = pltpu.SemaphoreType.DMA
    return pl.pallas_call(
        kernel,
        out_shape=jax.ShapeDtypeStruct((TOK, 1024), BF),
        in_specs=[pl.BlockSpec(memory_space=pl.ANY)] * 4 + [pl.BlockSpec(memory_space=pltpu.SMEM)],
        out_specs=pl.BlockSpec(memory_space=pltpu.VMEM),
        scratch_shapes=[
            pltpu.VMEM((2, TOK, GW), BF),
            pltpu.VMEM((6, TOK, 256), BF),
            pltpu.VMEM((6, TOK, 256), BF),
            pltpu.VMEM((2, TOK, NK), F32),
            pltpu.VMEM((2, 2, TOK, 2 * GW), BF),
            pltpu.VMEM((NT, 2 * GW, 256), BF),
            pltpu.VMEM((2, 2, NT, 2 * TOK, 128), BF),
            pltpu.VMEM((2, 2, NT - 1, 2 * TOK, 128), BF),
            pltpu.VMEM((2, 2, TOK, 128), BF),
            pltpu.VMEM((2, 2, TOK, 128), BF),
            pltpu.VMEM((2, 2, NC, 2, 32, 128), BF),
            pltpu.VMEM((2, 2, 2, NZ, 2, 32, 128), BF),
            pltpu.VMEM((2, 512, TOK), BF),
            pltpu.VMEM((TOK, 512), BF),
            pltpu.VMEM((NC, 2, 128), jnp.int32),
            pltpu.SMEM((NC, 2, 128), jnp.int32),
            dma((5,)),
            dma((NC,)), dma((NC,)),
            dma((1,)), dma((1,)),
            dma((5,)), dma((6,)),
            dma((8, 3)), dma((8, 3)),
            dma((3, 2, 4)), dma((3, 2, 4)),
            dma((2, 2, 2, 3)), dma((2, 2, 2, 3)),
            dma((2, 2)), dma((2, 2)),
            dma((2, 2, 2, NC)), dma((2, 2, 2, NC)),
        ],
        compiler_params=pltpu.CompilerParams(
            collective_id=0, has_side_effects=True, vmem_limit_bytes=56 * 1024 * 1024
        ),
        cost_estimate=pl.CostEstimate(flops=7_000_000_000, bytes_accessed=4_000_000, transcendentals=5_000_000),
    )(queries, key_value_vectors, out_weight, meta, doc_lengths)


def solution(mesh):
    placed = (
        P(("dp", "ctx"), "tp"),
        P(("dp", "ctx"), "tp"),
        P("tp", "ctx"),
        P("dp"),
        P(("dp", "ctx")),
    )
    return jax.shard_map(
        local, mesh=mesh, in_specs=placed, out_specs=P(("dp", "ctx"), "tp"), check_vma=False
    )
```

```python
import math

import jax
import jax.numpy as jnp
from jax import lax
from jax.experimental import pallas as pl
from jax.experimental.pallas import tpu as pltpu
from jax.sharding import PartitionSpec as P

MESH = pl.DeviceIdType.MESH
BF = jnp.bfloat16
F32 = jnp.float32
HS = 128
TOK = 256
GH = 8
GW = GH * HS
NK = 5 * TOK
SCALE = math.log2(math.e) / math.sqrt(HS)
NZ = 8
NC = 16
NT = 4
UP, DOWN = 3, 5
SHARED = 608
BOTH = 2 * GW - 2 * SHARED


def mult(value, of):
    return pl.multiple_of(value, of)


def kernel(
    q_ref, kv_ref, w_ref, meta_ref, len_ref, out_ref,
    qbuf, kvb, vo, bias, hbuf, wbuf, pbuf, rbuf, xsend, xrecv, sbuf, gbuf, sel, take, mbuf, msm,
    loc, m_s, m_r, q_s, q_r, kv_s, kv_r, w_s, w_r, h_s, h_r, y_s, y_r, x_s, x_r, g_s, g_r,
):
    x = lax.axis_index("dp")
    c = lax.axis_index("ctx")
    t = lax.axis_index("tp")
    z = c // 2
    k = lax.rem(c, 2)
    xp = lax.rem(x, 2)
    xq = x + 1 - 2 * xp
    sib = c + 1 - 2 * k
    xs = 3 - x
    half = lax.rem(x + x // 2, 2)
    upper = x // 2

    def remote(src, dst, send, recv, where):
        return pltpu.make_async_remote_copy(
            src_ref=src, dst_ref=dst, send_sem=send, recv_sem=recv, device_id=where, device_id_type=MESH
        )

    barrier = pltpu.get_barrier_semaphore()

    def greet_ctx(i, _):
        pl.semaphore_signal(barrier, inc=1, device_id={"ctx": lax.rem(c + i, NC)}, device_id_type=MESH)
        return 0

    lax.fori_loop(1, NC, greet_ctx, 0)
    for i in range(1, NT):
        pl.semaphore_signal(barrier, inc=1, device_id={"tp": lax.rem(t + i, NT)}, device_id_type=MESH)
    pl.semaphore_signal(barrier, inc=1, device_id={"dp": xq}, device_id_type=MESH)
    pl.semaphore_signal(barrier, inc=1, device_id={"dp": xs}, device_id_type=MESH)
    pl.semaphore_wait(barrier, NC - 1 + NT - 1 + 2)

    def kv_copy(i):
        if i == 0:
            g, slot, to = 1 - k, 4 + k, sib
        else:
            hop, g = (i + 1) // 2, (i + 1) % 2
            slot, to = 4 - 2 * hop + k, 2 * lax.rem(z + hop, NZ) + g
        return remote(
            kv_ref.at[:, pl.ds(mult(g * 256, 256), 256)], kvb.at[slot], kv_s.at[i], kv_r.at[slot], {"ctx": to}
        )

    def kv_arrival(slot):
        return remote(kvb.at[slot], kvb.at[slot], kv_s.at[0], kv_r.at[slot], {"ctx": sib})

    q_copy = remote(
        q_ref.at[:, pl.ds(mult((1 - k) * GW, GW), GW)], qbuf.at[k], q_s.at[0], q_r.at[0], {"ctx": sib}
    )
    q_arrival = remote(qbuf.at[1 - k], qbuf.at[1 - k], q_s.at[0], q_r.at[0], {"ctx": sib})

    def w_rows(j, mine=True):
        if j == 0:
            return pl.ds(mult((upper if mine else 1 - upper) * SHARED, 16), SHARED)
        return pl.ds(2 * SHARED, BOTH)

    def w_place(zz, rows):
        return wbuf.at[zz // 2, rows, pl.ds(mult(lax.rem(zz, 2) * 128, 128), 128)]

    def w_block(up, s):
        return lax.rem(z + (NZ - s if up else s), NZ)

    def w_index(up, s):
        return (0 if up else UP) + s - 1

    def w_copy(up, s, j):
        zz = w_block(up, s - 1)
        to = 2 * lax.rem(z + (1 if up else NZ - 1), NZ) + k
        n = w_index(up, s)
        place = w_place(zz, w_rows(j))
        src = w_ref.at[w_rows(j), pl.ds(mult(half * 128, 128), 128)] if s == 1 else place
        return remote(src, place, w_s.at[n, j], w_r.at[n, j], {"ctx": to})

    def w_share(up, s):
        n = w_index(up, s)
        place = w_place(w_block(up, s), w_rows(0))
        return remote(place, place, w_s.at[n, 2], w_r.at[n, 2], {"dp": xs})

    def w_shared(up, s):
        n = w_index(up, s)
        place = w_place(w_block(up, s), w_rows(0, False))
        return remote(place, place, w_s.at[n, 2], w_r.at[n, 2], {"dp": xs})

    def w_parts(up, s):
        return (1,) if up and s == UP else (0,) if not up and s == DOWN else (0, 1)

    def w_start(up, s, j):
        if s <= (UP if up else DOWN) and j in w_parts(up, s):
            w_copy(up, s, j).start()

    def w_arrived(up, s, j):
        n = w_index(up, s)
        place = w_place(w_block(up, s), w_rows(j))
        remote(place, place, w_s.at[n, j], w_r.at[n, j], {"ctx": sib}).wait_recv()
        w_start(up, s + 1, j)
        if j == 0:
            w_share(up, s).start()

    w_steps = [(True, s) for s in range(1, UP + 1)] + [(False, s) for s in range(1, DOWN + 1)]

    local_copies = [
        pltpu.make_async_copy(q_ref.at[:, pl.ds(mult(k * GW, GW), GW)], qbuf.at[k], loc.at[0]),
        pltpu.make_async_copy(kv_ref.at[:, pl.ds(mult(k * 256, 256), 256)], kvb.at[4 + k], loc.at[1]),
        pltpu.make_async_copy(w_ref.at[:, pl.ds(mult(half * 128, 128), 128)],
                              wbuf.at[z // 2, :, pl.ds(mult(lax.rem(z, 2) * 128, 128), 128)], loc.at[2]),
        pltpu.make_async_copy(meta_ref, mbuf.at[c], loc.at[3]),
    ]

    def m_copy(i):
        return remote(meta_ref, mbuf.at[c], m_s.at[i], m_r.at[i], {"ctx": lax.rem(c + i, NC)})

    kv_copy(0).start()
    w_copy(False, 1, 0).start()
    kv_copy(1).start()
    kv_copy(2).start()

    @pl.when(k == 1)
    def _():
        kv_copy(3).start()
        kv_copy(4).start()
        w_copy(True, 1, 0).start()

    @pl.when(k == 0)
    def _():
        w_copy(True, 1, 0).start()
        kv_copy(3).start()
        kv_copy(4).start()

    w_copy(False, 1, 1).start()
    w_copy(True, 1, 1).start()
    q_copy.start()
    for copy in local_copies:
        copy.start()

    def m_send(i, _):
        m_copy(i).start()
        return 0

    lax.fori_loop(1, NC, m_send, 0)

    ends = []
    total = jnp.int32(0)
    for d in range(8):
        total = total + len_ref[d]
        ends.append(total)
    for s in range(2):
        base = z * 512 + s * 256
        rows = lax.broadcasted_iota(jnp.int32, (TOK, 1), 0)
        start = jnp.zeros((TOK, 1), jnp.int32)
        for e in ends:
            start = jnp.where(rows + base >= e, e, start)
        keys = lax.broadcasted_iota(jnp.int32, (TOK, NK), 1)
        seen = (keys <= rows + 1024) & (keys >= start - (base - 1024))
        bias[s] = jnp.where(seen, 0.0, -1e30).astype(F32)

    kv_arrival(2).wait_recv()
    kv_arrival(3).wait_recv()

    for copy in local_copies:
        copy.wait()
    q_arrival.wait_recv()
    kv_arrival(5 - k).wait_recv()
    def widen(slot, count):
        vo[slot : slot + count, :, 0:HS] = kvb[slot : slot + count, :, HS:]
        vo[slot : slot + count, :, HS:] = jnp.ones((count, TOK, HS), BF)

    widen(2, 4)
    w_arrived(False, 1, 0)
    w_arrived(False, 1, 1)
    kv_arrival(1).wait_recv()
    widen(1, 1)

    def h_lanes(j, kk):
        return pl.ds(mult(kk * GW + j * 256, 256), 256)

    def h_to_partner(s, j):
        return remote(hbuf.at[0, s, :, h_lanes(j, k)], hbuf.at[1, s, :, h_lanes(j, k)],
                      h_s.at[0, s, j], h_r.at[0, s, j], {"dp": xq})

    def h_to_sibling(s, j):
        place = hbuf.at[0, s, :, h_lanes(j, k)]
        return remote(place, place, h_s.at[1, s, j], h_r.at[1, s, j], {"ctx": sib})

    def h_forward(s, j):
        place = hbuf.at[1, s, :, h_lanes(j, k)]
        return remote(place, place, h_s.at[2, s, j], h_r.at[2, s, j], {"ctx": sib})

    def h_arrival(s, j, way):
        place = hbuf.at[1, s, :, h_lanes(j, k)] if way == 0 else hbuf.at[way - 1, s, :, h_lanes(j, 1 - k)]
        return remote(place, place, h_s.at[way, s, j], h_r.at[way, s, j], {"ctx": sib})

    def attend(s, j):
        keys = kvb[s : s + 5, :, 0:HS].reshape(NK, HS)
        values = vo[s : s + 5].reshape(NK, 2 * HS)
        heads = (2 * j, 2 * j + 1)
        scores = [
            lax.dot_general(qbuf[s, :, h * HS : (h + 1) * HS], keys, (((1,), (1,)), ((), ())),
                            preferred_element_type=F32)
            for h in heads
        ]
        for h, score in zip(heads, scores):
            score = score * SCALE + bias[s]
            weights = jnp.exp2(score - jnp.max(score, axis=1, keepdims=True)).astype(BF)
            mixed = jnp.dot(weights, values, preferred_element_type=F32)
            hbuf[0, s, :, pl.ds(mult(k * GW + h * HS, HS), HS)] = (mixed[:, :HS] / mixed[:, HS:]).astype(BF)
        h_to_partner(s, j).start()
        h_to_sibling(s, j).start()

    def h_pass_on(s, j):
        h_arrival(s, j, 0).wait_recv()
        h_forward(s, j).start()

    attend(1, 0)
    w_arrived(False, 2, 0)
    attend(1, 1)
    w_arrived(False, 2, 1)
    attend(1, 2)
    attend(1, 3)
    w_arrived(True, 1, 0)
    w_arrived(False, 3, 0)
    kv_arrival(0).wait_recv()
    widen(0, 1)
    attend(0, 0)
    h_pass_on(1, 0)
    attend(0, 1)
    w_arrived(False, 3, 1)
    w_arrived(True, 1, 1)
    h_pass_on(1, 1)
    attend(0, 2)
    h_pass_on(1, 2)
    attend(0, 3)
    w_arrived(False, 4, 0)
    w_arrived(True, 2, 0)
    h_pass_on(1, 3)

    def m_wait(i, _):
        src = lax.rem(c + NC - i, NC)
        remote(mbuf.at[src], mbuf.at[src], m_s.at[i], m_r.at[i], {"ctx": sib}).wait_recv()
        return 0

    lax.fori_loop(1, NC, m_wait, 0)
    table = pltpu.make_async_copy(mbuf, msm, loc.at[4])
    table.start()
    table.wait()

    def owner(n, b):
        return msm[n, b // 8, (b % 8) * 16]

    lane = lax.broadcasted_iota(jnp.int32, (1, TOK), 1)
    for s in range(2):
        owners = [owner(2 * z + s, b) for b in range(16)]
        wanted = jnp.zeros((1, TOK), jnp.int32)
        for b in range(16):
            second = jnp.int32(0)
            for e in range(b):
                second = second + jnp.where(owners[e] == owners[b], 16, 0)
            slot = owners[b] - c
            slot = jnp.where(slot < 0, slot + NC, slot)
            wanted = jnp.where(lane // 16 == b, slot * 32 + second, wanted)
        wanted = wanted + lax.rem(lane, 16)
        row = lax.broadcasted_iota(jnp.int32, (512, TOK), 0)
        sel[s] = jnp.where(row == wanted, 1.0, 0.0).astype(BF)

    counts = []
    count = jnp.int32(0)
    for n in range(NC):
        any_block = jnp.int32(0)
        for b in range(16):
            any_block = jnp.maximum(any_block, jnp.where(owner(n, b) == c, 1, 0))
        count = count + any_block
        counts.append(count)

    def place(r, _):
        src = jnp.int32(0)
        for n in range(NC - 1):
            src = src + jnp.where(counts[n] <= r, 1, 0)
        row = lax.broadcasted_iota(jnp.int32, (32, 512), 0)
        column = lax.broadcasted_iota(jnp.int32, (32, 512), 1)
        take[pl.ds(mult(r * 32, 32), 32), :] = jnp.where(column == row + src * 32, 1.0, 0.0).astype(BF)
        return 0

    lax.fori_loop(0, 8, place, 0)

    def column_half(o):
        return lax.rem(z + o, 2)

    def piece(e, s):
        return pl.ds(s * TOK, TOK) if e == 1 else pl.ds(0, 2 * TOK)

    pieces = ((0, 0), (1, 0), (1, 1))

    def y_copy(o, e, s, i):
        tt = lax.rem(t + 1 + i, NT)
        return remote(pbuf.at[o, e, tt, piece(e, s)], rbuf.at[o, e, i, piece(e, s)],
                      y_s.at[o, e, s, i], y_r.at[o, e, s, i], {"tp": tt})

    def product(o, e):
        def one(i, _):
            tt = lax.rem(t + 1 + i, NT)
            columns = wbuf[tt, :, pl.ds(mult(column_half(o) * 128, 128), 128)]
            part = jnp.dot(hbuf[e].reshape(2 * TOK, 2 * GW), columns, preferred_element_type=F32)
            pbuf[o, e, tt] = part.astype(BF)

            @pl.when(i < NT - 1)
            def _():
                y_copy(o, e, 0, i).start()

            return 0

        lax.fori_loop(0, NT, one, 0)
        if e == 1:
            for i in range(NT - 1):
                y_copy(o, e, 1, i).start()

    def summed(o, e, s):
        total = pbuf[o, e, t, piece(e, s)].astype(F32)
        for i in range(NT - 1):
            place = rbuf.at[o, e, i, piece(e, s)]
            remote(place, place, y_s.at[o, e, s, i], y_r.at[o, e, s, i], {"ctx": sib}).wait_recv()
            total = total + rbuf[o, e, i, piece(e, s)].astype(F32)
        return total.astype(BF)

    def x_return(o, s):
        return remote(xsend.at[o, s], xrecv.at[o, s], x_s.at[o, s], x_r.at[o, s], {"dp": xq})

    def shards(e, s):
        return pl.ds(s, 1) if e == 1 else pl.ds(0, 2)

    def g_copy(o, e, s, i):
        a = column_half(o)
        return remote(sbuf.at[o, e, i, shards(e, s)], gbuf.at[k, a, e, z, shards(e, s)],
                      g_s.at[a, e, s, i], g_r.at[a, e, s, i], {"ctx": lax.rem(c + i, NC)})

    def pick(o, e, s, rows):
        picked = jnp.dot(sel[s], rows, preferred_element_type=F32)
        sbuf[o, e, :, s] = picked.astype(BF).reshape(NC, 32, 128)

    def send_packed(o, e, s):
        def send(i, _):
            g_copy(o, e, s, i).start()
            return 0

        lax.fori_loop(1, NC, send, 0)
        gbuf[k, column_half(o), e, z, shards(e, s)] = sbuf[o, e, 0, shards(e, s)]

    def pack(o):
        rows = summed(o, 0, 0)
        for s in range(2):
            pick(o, 0, s, rows[s * TOK : (s + 1) * TOK])
        send_packed(o, 0, 0)

    def give_back(o, s):
        xsend[o, s] = summed(o, 1, s)
        x_return(o, s).start()

    def pack_returned(o, s):
        x_return(o, s).wait_recv()
        pick(o, 1, s, xrecv[o, s])
        send_packed(o, 1, s)

    w_arrived(False, 4, 1)
    w_arrived(True, 2, 1)
    for up, s in w_steps:
        if s % 2 == 0:
            w_shared(up, s).wait_recv()
    for s in range(2):
        for j in range(4):
            h_arrival(s, j, 1).wait_recv()
    h_pass_on(0, 0)
    product(0, 0)
    h_pass_on(0, 1)
    w_arrived(False, 5, 0)
    w_arrived(True, 3, 1)
    h_pass_on(0, 2)
    h_pass_on(0, 3)
    for s in range(2):
        for j in range(4):
            h_arrival(s, j, 2).wait_recv()
    product(0, 1)
    for up, s in w_steps:
        if s % 2 == 1 and 0 in w_parts(up, s):
            w_shared(up, s).wait_recv()
    pack(0)
    product(1, 0)
    give_back(0, 0)
    give_back(0, 1)
    pack_returned(0, 0)
    product(1, 1)
    pack_returned(0, 1)
    pack(1)
    give_back(1, 0)
    give_back(1, 1)
    pack_returned(1, 0)
    pack_returned(1, 1)

    for i in range(5):
        kv_copy(i).wait_send()
    q_copy.wait_send()
    for up, s in w_steps:
        for j in w_parts(up, s):
            w_copy(up, s, j).wait_send()
            if j == 0:
                w_share(up, s).wait_send()
    for s in range(2):
        for j in range(4):
            h_to_partner(s, j).wait_send()
            h_to_sibling(s, j).wait_send()
            h_forward(s, j).wait_send()
    for o in range(2):
        for s in range(2):
            x_return(o, s).wait_send()
        for e, s in pieces:
            for i in range(NT - 1):
                y_copy(o, e, s, i).wait_send()

    def sent(i, _):
        m_copy(i).wait_send()
        for e, s in pieces:
            g_copy(0, e, s, i).wait_send()
        return 0

    lax.fori_loop(1, NC, sent, 0)

    for e in range(2):
        for a in range(2):
            def g_wait(i, _):
                src = lax.rem(c + NC - i, NC)
                for s in range(2 if e == 1 else 1):
                    place = gbuf.at[lax.rem(src, 2), a, e, src // 2, shards(e, s)]
                    remote(place, place, g_s.at[a, e, s, i], g_r.at[a, e, s, i], {"ctx": sib}).wait_recv()
                return 0

            lax.fori_loop(1, NC, g_wait, 0)
            for kk in range(2):
                rows = jnp.dot(take[...], gbuf[kk, a, e].reshape(2 * TOK, 128), preferred_element_type=F32)
                at = a * 512 + kk * 256 + (half if e == 0 else 1 - half) * 128
                out_ref[:, pl.ds(mult(at, 128), 128)] = rows.astype(BF)

    def sent_last(i, _):
        for e, s in pieces:
            g_copy(1, e, s, i).wait_send()
        return 0

    lax.fori_loop(1, NC, sent_last, 0)


def local(queries, key_value_vectors, out_weight, doc_lengths, shard_of):
    meta = shard_of.reshape(2, 128)
    dma = pltpu.SemaphoreType.DMA
    return pl.pallas_call(
        kernel,
        out_shape=jax.ShapeDtypeStruct((TOK, 1024), BF),
        in_specs=[pl.BlockSpec(memory_space=pl.ANY)] * 4 + [pl.BlockSpec(memory_space=pltpu.SMEM)],
        out_specs=pl.BlockSpec(memory_space=pltpu.VMEM),
        scratch_shapes=[
            pltpu.VMEM((2, TOK, GW), BF),
            pltpu.VMEM((6, TOK, 256), BF),
            pltpu.VMEM((6, TOK, 256), BF),
            pltpu.VMEM((2, TOK, NK), F32),
            pltpu.VMEM((2, 2, TOK, 2 * GW), BF),
            pltpu.VMEM((NT, 2 * GW, 256), BF),
            pltpu.VMEM((2, 2, NT, 2 * TOK, 128), BF),
            pltpu.VMEM((2, 2, NT - 1, 2 * TOK, 128), BF),
            pltpu.VMEM((2, 2, TOK, 128), BF),
            pltpu.VMEM((2, 2, TOK, 128), BF),
            pltpu.VMEM((2, 2, NC, 2, 32, 128), BF),
            pltpu.VMEM((2, 2, 2, NZ, 2, 32, 128), BF),
            pltpu.VMEM((2, 512, TOK), BF),
            pltpu.VMEM((TOK, 512), BF),
            pltpu.VMEM((NC, 2, 128), jnp.int32),
            pltpu.SMEM((NC, 2, 128), jnp.int32),
            dma((5,)),
            dma((NC,)), dma((NC,)),
            dma((1,)), dma((1,)),
            dma((5,)), dma((6,)),
            dma((8, 3)), dma((8, 3)),
            dma((3, 2, 4)), dma((3, 2, 4)),
            dma((2, 2, 2, 3)), dma((2, 2, 2, 3)),
            dma((2, 2)), dma((2, 2)),
            dma((2, 2, 2, NC)), dma((2, 2, 2, NC)),
        ],
        compiler_params=pltpu.CompilerParams(
            collective_id=0, has_side_effects=True, vmem_limit_bytes=56 * 1024 * 1024
        ),
        cost_estimate=pl.CostEstimate(flops=7_000_000_000, bytes_accessed=4_000_000, transcendentals=5_000_000),
    )(queries, key_value_vectors, out_weight, meta, doc_lengths)


def solution(mesh):
    placed = (
        P(("dp", "ctx"), "tp"),
        P(("dp", "ctx"), "tp"),
        P("tp", "ctx"),
        P("dp"),
        P(("dp", "ctx")),
    )
    return jax.shard_map(
        local, mesh=mesh, in_specs=placed, out_specs=P(("dp", "ctx"), "tp"), check_vma=False
    )
```
